256 devices in a mesh: dp: 16 (over y, z_hi, core), proto: 16 (over z_lo, x).
Axes of the slice: x: 4, y: 4, z: 8 (z_hi: 2, z_lo: 4; z = z_hi * 4 + z_lo), core: 2. Of those that a mesh axis runs over, the one named last changes fastest.
Arguments:
- teacher_hidden: bfloat16 [12288, 2048], P('dp', 'proto'), may hold values from -4 to 7
- student_hidden: bfloat16 [12288, 2048], P('dp', 'proto'), may hold values from -6 to 6
- teacher_bottleneck: bfloat16 [2048, 256], P('proto'), may hold values from -1 to 1
- student_bottleneck: bfloat16 [2048, 256], P('proto'), may hold values from -0.125 to 0.125
- teacher_prototypes: bfloat16 [256, 65536], P(None, 'proto'), may hold values from -7 to 7
- student_prototypes: bfloat16 [256, 65536], P(None, 'proto'), may hold values from -0.375 to 0.375
Outputs:
- grad_prototypes: float32 [256, 65536], P('dp', 'proto')
- grad_bottleneck: float32 [2048, 256], P('proto', 'dp')
The draws below stay inside these ranges and needn't reach their ends.
All inputs are finite; a program needn't handle non-finite values.
Results may differ from the reference program's by a relative error of at most 0.012.
Values may be sent and summed in bfloat16 or wider, within the bound.
No kernel may reach another device: no remote copies, remote signals or barrier semaphores. Data moves between devices by JAX's collectives and lax.ppermute only.
A program may use at most 128 MiB of HBM per device.

```python
import jax
import jax.numpy as jnp
from jax import lax

HID = 2048
BOT = 256
PROTOS = 65536
ITERS = 3
CROPS = 12288
N_PROTO = 16


def shared_clusters(key):
    groups = 8
    coords = jax.random.permutation(jax.random.fold_in(key, 101), HID)[:groups].astype(jnp.int32)
    direct = jnp.clip(jax.random.normal(jax.random.fold_in(key, 102), (groups, BOT), jnp.float32), -3.0, 3.0)
    return (coords, direct)


def member_of(member_key, count, flipped):
    groups = 8
    picked = jax.random.randint(member_key, (count,), 0, 36, dtype=jnp.int32)
    levels = jnp.arange(1, groups, dtype=jnp.int32)
    bounds = levels * (levels + 1) // 2
    member = jnp.sum((picked[:, None] >= bounds[None, :]).astype(jnp.int32), axis=1)
    return flipped * (groups - 1) + (1 - 2 * flipped) * member


def draw_teacher_hidden(key, part):
    coords, direct = shared_clusters(key)
    key = jax.random.fold_in(key, 1)
    member = member_of(jax.random.fold_in(key, 11), CROPS, 0)
    jitter = jnp.clip(jax.random.normal(jax.random.fold_in(key, 12), (CROPS, HID), jnp.float32), -4.0, 4.0)
    strength = jax.random.uniform(jax.random.fold_in(key, 13), (CROPS,), jnp.float32, 3.5, 7.0)
    target = coords[member]
    on_spot = jnp.arange(HID, dtype=jnp.int32)[None, :] == target[:, None]
    return jnp.where(on_spot, strength[:, None], jitter).astype(jnp.bfloat16)


def draw_teacher_bottleneck(key, part):
    coords, direct = shared_clusters(key)
    key = jax.random.fold_in(key, 2)
    spread = jnp.clip(jax.random.normal(key, (HID, BOT), jnp.float32), -6.0, 6.0) / HID ** 0.5
    return spread.at[coords].set(direct / 3.0).astype(jnp.bfloat16)


def draw_teacher_prototypes(key, part):
    coords, direct = shared_clusters(key)
    key = jax.random.fold_in(key, 3)
    member = member_of(jax.random.fold_in(key, 11), PROTOS, 1)
    jitter = jnp.clip(jax.random.normal(jax.random.fold_in(key, 12), (BOT, PROTOS), jnp.float32), -4.0, 4.0)
    strength = jax.random.uniform(jax.random.fold_in(key, 13), (PROTOS,), jnp.float32, 0.5, 1.0)
    return (strength[None, :] * direct[member].T + jitter).astype(jnp.bfloat16)


def block_scale(stream_key, extent, split, least, top_value):
    level = 1.0
    for axis_at, shards_of in split:
        steps = jax.random.uniform(jax.random.fold_in(jax.random.fold_in(stream_key, 6), axis_at), (shards_of,), jnp.float32, least / len(split), top_value / len(split))
        level = level * jnp.repeat(jnp.exp(steps), extent[axis_at] // shards_of).reshape((-1,) + (1,) * (len(extent) - 1 - axis_at))
    return level


def bell_draw(rng, extent, deviation, limit, cuts=(), held_as=jnp.bfloat16):
    factor_of = block_scale(rng, extent, cuts, -0.22, 0.18) if cuts else 1.0
    values = jax.random.normal(rng, extent, jnp.float32) * deviation * factor_of
    return jnp.minimum(jnp.maximum(values, -limit), limit).astype(held_as)


def setup_inputs(seed: int = 0) -> dict:
    key_list = jax.random.split(jax.random.key(seed), 7)
    return {
        "teacher_hidden": draw_teacher_hidden(jax.random.fold_in(key_list[6], 71), 0),
        "student_hidden": bell_draw(key_list[1], (CROPS, HID), 1.0, 6.0, ((0, 16), (1, 16))),
        "teacher_bottleneck": draw_teacher_bottleneck(jax.random.fold_in(key_list[6], 71), 0),
        "student_bottleneck": bell_draw(key_list[3], (HID, BOT), HID ** -0.5, 0.125, ((0, 16),)),
        "teacher_prototypes": draw_teacher_prototypes(jax.random.fold_in(key_list[6], 71), 0),
        "student_prototypes": bell_draw(key_list[5], (BOT, PROTOS), BOT ** -0.5, 0.375, ((1, 16),)),
    }


TEACHER_TEMP = 0.07
STUDENT_TEMP = 0.1
EPSILON = 1e-06

def unit_rows(values):
    scale = lax.rsqrt(lax.optimization_barrier(jnp.sum(values * values, axis=1, keepdims=True)) + EPSILON)
    return (values * scale, scale)

def unit_cols(weights):
    values = weights.astype(jnp.float32)
    scale = lax.rsqrt(lax.optimization_barrier(jnp.sum(values * values, axis=0, keepdims=True)) + EPSILON)
    return (values * scale, scale)

def reference(teacher_hidden, student_hidden, teacher_bottleneck, student_bottleneck, teacher_prototypes, student_prototypes):
    teach_proj = jnp.dot(teacher_hidden, teacher_bottleneck, preferred_element_type=jnp.float32)
    stud_proj = jnp.dot(student_hidden, student_bottleneck, preferred_element_type=jnp.float32)
    teach_unit, unused_scale = unit_rows(teach_proj)
    stud_unit, stud_scale = unit_rows(stud_proj)
    teach_low = teach_unit.astype(jnp.bfloat16)
    stud_low = stud_unit.astype(jnp.bfloat16)
    teach_norm, unused_cols = unit_cols(teacher_prototypes)
    stud_norm, col_norm = unit_cols(student_prototypes)
    blocks = N_PROTO
    width = PROTOS // N_PROTO
    teach_blocks = teach_norm.astype(jnp.bfloat16).reshape(BOT, blocks, width).transpose(1, 0, 2)
    stud_blocks = stud_norm.astype(jnp.bfloat16).reshape(BOT, blocks, width).transpose(1, 0, 2)

    def teacher_expo(block):
        return jnp.exp(jnp.dot(teach_low, block, preferred_element_type=jnp.float32) / TEACHER_TEMP)

    def student_expo(block):
        return jnp.exp(jnp.dot(stud_low, block, preferred_element_type=jnp.float32) / STUDENT_TEMP)
    row_scale = jnp.ones((CROPS,), jnp.float32)
    col_scale = jnp.ones((blocks, width), jnp.float32)
    for step in range(ITERS):
        current = row_scale

        def sweep(accum, block):
            expo = teacher_expo(block)
            cols = 1.0 / jnp.dot(current, expo, precision=lax.Precision.HIGHEST)
            return (accum + jnp.dot(expo, cols, precision=lax.Precision.HIGHEST), cols)
        accum, col_scale = lax.scan(sweep, jnp.zeros((CROPS,), jnp.float32), teach_blocks)
        row_scale = 1.0 / accum

    def add_totals(accum, block):
        return (accum + lax.optimization_barrier(jnp.sum(student_expo(block), axis=1)), None)
    totals, unused_none = lax.scan(add_totals, jnp.zeros((CROPS,), jnp.float32), stud_blocks)
    factor = PROTOS / 32.0

    def backward(feat_grad, pieces):
        teach_block, stud_block, cols = pieces
        assign = row_scale[:, None] * teacher_expo(teach_block) * cols[None, :]
        probs = student_expo(stud_block) / totals[:, None]
        logit_grad = (factor * (probs - assign) / STUDENT_TEMP).astype(jnp.bfloat16)
        proto_part = lax.dot_general(stud_low, logit_grad, (((0,), (0,)), ((), ())), preferred_element_type=jnp.float32)
        feat_part = lax.dot_general(logit_grad, stud_block, (((1,), (1,)), ((), ())), preferred_element_type=jnp.float32)
        return (feat_grad + feat_part, proto_part)
    feat_grad, proto_parts = lax.scan(backward, jnp.zeros((CROPS, BOT), jnp.float32), (teach_blocks, stud_blocks, col_scale))
    proto_sum = proto_parts.transpose(1, 0, 2).reshape(BOT, PROTOS)
    dots = lax.optimization_barrier(jnp.sum(stud_norm * proto_sum, axis=0, keepdims=True))
    grad_prototypes = col_norm * (proto_sum - stud_norm * dots)
    inner = lax.optimization_barrier(jnp.sum(stud_unit * feat_grad, axis=1, keepdims=True))
    proj_grad = (stud_scale * (feat_grad - stud_unit * inner)).astype(jnp.bfloat16)
    grad_bottleneck = lax.dot_general(student_hidden, proj_grad, (((0,), (0,)), ((), ())), preferred_element_type=jnp.float32)
    return (grad_prototypes, grad_bottleneck)
```

```python
import jax
import jax.numpy as jnp
from jax import lax
from jax.sharding import PartitionSpec as P

PROTOS = 65536
ITERS = 3


TEACHER_TEMP = 0.07
STUDENT_TEMP = 0.1
EPSILON = 1e-06

Y_GROUPS = [[y * 4 + z * 2 + c for y in range(4)] for z in range(2) for c in range(2)]


def unit_rows(values):
    scale = lax.rsqrt(jnp.sum(values * values, axis=1, keepdims=True) + EPSILON)
    return (values * scale, scale)


def unit_cols(weights):
    values = weights.astype(jnp.float32)
    scale = lax.rsqrt(jnp.sum(values * values, axis=0, keepdims=True) + EPSILON)
    return (values * scale, scale)


def scatter_rows(part, axis, groups=None):
    count = lax.axis_size(axis) if groups is None else len(groups[0])
    blocks = part.astype(jnp.bfloat16).reshape((count, part.shape[0] // count) + part.shape[1:])
    got = lax.all_to_all(blocks, axis, 0, 0, tiled=True, axis_index_groups=groups)
    return jnp.sum(got.astype(jnp.float32), axis=0)


def gather_all(share, axis):
    count = lax.axis_size(axis)
    copies = jnp.broadcast_to(share[None], (count,) + share.shape)
    return lax.all_to_all(copies, axis, 0, 0, tiled=True)


def gather_rows(share, axis):
    got = gather_all(share, axis)
    return got.reshape((-1,) + share.shape[1:])


def sum_over(vector, axis):
    return jnp.sum(gather_all(vector.reshape(-1, 128), axis), axis=0).reshape(vector.shape)


def on_device(
    teacher_hidden,
    student_hidden,
    teacher_bottleneck,
    student_bottleneck,
    teacher_prototypes,
    student_prototypes,
):
    teach_part = jnp.dot(teacher_hidden, teacher_bottleneck, preferred_element_type=jnp.float32)
    stud_part = jnp.dot(student_hidden, student_bottleneck, preferred_element_type=jnp.float32)
    both = jnp.concatenate([teach_part, stud_part], axis=1)
    share = scatter_rows(both, "proto")
    teach_unit, unused_scale = unit_rows(share[:, :256])
    stud_unit_rows, stud_scale_rows = unit_rows(share[:, 256:])
    low = jnp.concatenate(
        [teach_unit.astype(jnp.bfloat16), stud_unit_rows.astype(jnp.bfloat16)], axis=1
    )
    low = gather_rows(low, "proto")
    teach_low = low[:, :256]
    stud_low = low[:, 256:]
    teach_norm, unused_cols = unit_cols(teacher_prototypes)
    stud_norm, col_norm = unit_cols(student_prototypes)
    teach_wlow = teach_norm.astype(jnp.bfloat16)
    stud_wlow = stud_norm.astype(jnp.bfloat16)
    expo = jnp.exp(
        jnp.dot(teach_low, teach_wlow, preferred_element_type=jnp.float32) / TEACHER_TEMP
    )
    stud_expo = jnp.exp(
        jnp.dot(stud_low, stud_wlow, preferred_element_type=jnp.float32) / STUDENT_TEMP
    )
    totals_part = jnp.sum(stud_expo, axis=1)
    row_scale = jnp.ones((expo.shape[0],), jnp.float32)
    for step in range(ITERS):
        col_part = jnp.sum(expo * row_scale[:, None], axis=0)
        col_scale = 1.0 / sum_over(col_part, "dp")
        row_part = jnp.sum(expo * col_scale[None, :], axis=1)
        if step == 0:
            sums = sum_over(jnp.concatenate([row_part, totals_part]), "proto")
            row_scale = 1.0 / sums[: expo.shape[0]]
            totals = sums[expo.shape[0] :]
        else:
            row_scale = 1.0 / sum_over(row_part, "proto")
    factor = PROTOS / 32.0
    assign = row_scale[:, None] * expo * col_scale[None, :]
    logit_grad = (factor * (stud_expo / totals[:, None] - assign) / STUDENT_TEMP).astype(
        jnp.bfloat16
    )
    feat_part = lax.dot_general(
        logit_grad, stud_wlow, (((1,), (1,)), ((), ())), preferred_element_type=jnp.float32
    )
    proto_part = lax.dot_general(
        stud_low, logit_grad, (((0,), (0,)), ((), ())), preferred_element_type=jnp.float32
    )
    dots = jnp.sum(stud_norm * proto_part, axis=0, keepdims=True)
    grad_part = col_norm * (proto_part - stud_norm * dots)

    feat_grad = scatter_rows(feat_part, "proto")
    inner = jnp.sum(stud_unit_rows * feat_grad, axis=1, keepdims=True)
    proj_share = (stud_scale_rows * (feat_grad - stud_unit_rows * inner)).astype(jnp.bfloat16)
    proj_grad = gather_rows(proj_share, "proto")
    bottle_part = lax.dot_general(
        proj_grad, student_hidden, (((0,), (0,)), ((), ())), preferred_element_type=jnp.float32
    )
    grad_bottleneck = scatter_rows(bottle_part, "dp").T

    where = lax.axis_index("dp")
    core = where % 2
    high = (where // 2) % 2
    blocks = grad_part.reshape(4, 2, 2, 16, -1)
    keep = jnp.where(core == 0, blocks[:, :, 0], blocks[:, :, 1])
    send = jnp.where(core == 0, blocks[:, :, 1], blocks[:, :, 0]).astype(jnp.bfloat16)
    got = lax.ppermute(send, "dp", [(i, i ^ 1) for i in range(16)])
    pair = keep + got.astype(jnp.float32)
    quarter = scatter_rows(pair, "dp", Y_GROUPS)[0]
    keep = jnp.where(high == 0, quarter[0], quarter[1])
    send = jnp.where(high == 0, quarter[1], quarter[0]).astype(jnp.bfloat16)
    got = lax.ppermute(send, "dp", [(i, i ^ 2) for i in range(16)])
    grad_prototypes = keep + got.astype(jnp.float32)
    return (grad_prototypes, grad_bottleneck)


def solution(mesh):
    return jax.shard_map(
        on_device,
        mesh=mesh,
        in_specs=(
            P("dp", "proto"),
            P("dp", "proto"),
            P("proto", None),
            P("proto", None),
            P(None, "proto"),
            P(None, "proto"),
        ),
        out_specs=(P("dp", "proto"), P("proto", "dp")),
        check_vma=False,
    )
```

```python
import jax
import jax.numpy as jnp
from jax import lax
from jax.experimental import pallas as pl
from jax.experimental.pallas import tpu as pltpu
from jax.sharding import PartitionSpec as P

PROTOS = 65536
ITERS = 3

TEACHER_TEMP = 0.07
STUDENT_TEMP = 0.1
EPSILON = 1e-06
LOG2E = 1.4426950408889634

LANES = 128
WIDE = 512
LIMIT = 16 * 2**20
KEEP = jnp.float32
BLOCK = 16


def unit_rows(values):
    scale = lax.rsqrt(jnp.sum(values * values, axis=1, keepdims=True) + EPSILON)
    return (values * scale, scale)


def col_scales(weights):
    values = weights.astype(jnp.float32)
    return lax.rsqrt(jnp.sum(values * values, axis=0, keepdims=True) + EPSILON)


def on_core(kernel, outs, args, scratch=(), pinned=(), smem=(), far=(), far_outs=()):
    args = [
        pltpu.with_memory_space_constraint(a, pltpu.VMEM if i in pinned else pltpu.HBM)
        if i in pinned or i in far
        else a
        for i, a in enumerate(args)
    ]

    def place(i, far_ones):
        return pl.BlockSpec(memory_space=pltpu.HBM if i in far_ones else pltpu.VMEM)

    return pl.pallas_call(
        kernel,
        out_shape=tuple(outs),
        in_specs=[
            pl.BlockSpec(memory_space=pltpu.SMEM) if i in smem else place(i, far)
            for i in range(len(args))
        ],
        out_specs=tuple(place(i, far_outs) for i in range(len(outs))),
        scratch_shapes=list(scratch),
        compiler_params=pltpu.CompilerParams(vmem_limit_bytes=LIMIT),
    )(*args)


def fetch(far_ref, near_ref, sems):
    copies = []
    for k in range(far_ref.shape[1] // WIDE):
        cols = pl.ds(k * WIDE, WIDE)
        copies.append(pltpu.make_async_copy(far_ref.at[:, cols], near_ref.at[:, cols], sems.at[k]))
        copies[-1].start()
    return copies


def column_of(rows, j):
    return jnp.broadcast_to(rows[j : j + 1, :], (LANES, LANES)).T


def put_row_sums(acc_ref, out_ref, sums_ref):
    sums_ref[...] = jnp.zeros_like(sums_ref)
    for j in range(acc_ref.shape[0] // LANES):
        sums_ref[pl.ds(j, 1), :] = jnp.sum(
            acc_ref[pl.ds(j * LANES, LANES), :].T, axis=0, keepdims=True
        )
    sums = sums_ref[...]
    high = sums.astype(jnp.bfloat16).astype(jnp.float32)
    block = jnp.concatenate([high, sums - high], axis=0).astype(jnp.bfloat16)
    for p in range(out_ref.shape[0]):
        out_ref[p, pl.ds(0, BLOCK), :] = block


def get_row_sums(got_ref, first):
    terms = jnp.sum(got_ref[:, pl.ds(first, BLOCK), :].astype(jnp.float32), axis=0)
    return terms[:8] + terms[8:]


def diagonal(rows, columns):
    shape = (rows, columns)
    return lax.broadcasted_iota(jnp.int32, shape, 0) == lax.broadcasted_iota(jnp.int32, shape, 1)


def share_kernel(got_ref, out_ref):
    unit, unused_scale = unit_rows(jnp.sum(got_ref[...].astype(jnp.float32), axis=0))
    unit = unit.astype(out_ref.dtype)
    for p in range(out_ref.shape[0]):
        out_ref[p] = unit


def proj_kernel(got_ref, share_ref, out_ref):
    unit, scale = unit_rows(share_ref[...])
    share, width = unit.shape
    got = jnp.sum(got_ref[...].astype(jnp.float32), axis=0)
    along = jnp.where(diagonal(share, width), got[share : share + 1], 0.0)
    low = unit.astype(jnp.bfloat16).astype(jnp.float32)
    feat = got[:share] + low * jnp.sum(along, axis=1, keepdims=True)
    inner = jnp.sum(unit * feat, axis=1, keepdims=True)
    rows = (scale * (feat - unit * inner)).astype(out_ref.dtype)
    for p in range(out_ref.shape[0]):
        out_ref[p] = rows


def teacher_kernel(low_ref, w_far, expo_ref, out_ref, w_ref, sems, sums_ref):
    loads = fetch(w_far, w_ref, sems)
    low = low_ref[...]
    for k in range(w_ref.shape[1] // WIDE):
        cols = pl.ds(k * WIDE, WIDE)
        loads[k].wait()
        scores = jnp.dot(low, w_ref[:, cols], preferred_element_type=jnp.float32)
        expo = jnp.exp2(scores * (LOG2E / TEACHER_TEMP))
        expo_ref[:, cols] = expo.astype(expo_ref.dtype)
        sums = jnp.sum(expo, axis=0, keepdims=True)
        for t in range(WIDE // LANES):
            sums_ref[pl.ds(k * (WIDE // LANES) + t, 1), :] = sums[:, t * LANES : (t + 1) * LANES]
    sums = sums_ref[...].astype(out_ref.dtype)
    for p in range(out_ref.shape[0]):
        out_ref[p] = sums


def student_kernel(got_ref, w_ref, expo_ref, totals_ref, low_ref, acc_ref, sums_ref):
    share = (got_ref.shape[1] - BLOCK) // 2
    for p in range(got_ref.shape[0]):
        for half in range(2):
            low_ref[pl.ds(p * share, share), pl.ds(half * LANES, LANES)] = got_ref[
                p, pl.ds(BLOCK + half * share, share), :
            ]
    low = low_ref[...]
    for k in range(w_ref.shape[1] // WIDE):
        cols = pl.ds(k * WIDE, WIDE)
        scores = jnp.dot(low, w_ref[:, cols], preferred_element_type=jnp.float32)
        expo = jnp.exp2(scores * (LOG2E / STUDENT_TEMP))
        expo_ref[:, cols] = expo.astype(expo_ref.dtype)
        part = sum(expo[:, t * LANES : (t + 1) * LANES] for t in range(WIDE // LANES))
        acc_ref[...] = part if k == 0 else acc_ref[...] + part
    put_row_sums(acc_ref, totals_ref, sums_ref)


def row_kernel(expo_ref, got_ref, *refs):
    extra_ref = refs[0] if len(refs) == 5 else None
    out_ref, scale_ref, acc_ref, sums_ref = refs[-4:]
    rows, columns = expo_ref.shape
    scale_ref[...] = 1.0 / jnp.sum(got_ref[...].astype(jnp.float32), axis=0)
    block = 64

    def body(i, _):
        at = pl.multiple_of(i * block, block)
        acc = [jnp.zeros((8, LANES), jnp.float32)] * (block // 8)
        for t in range(columns // LANES):
            scale = jnp.broadcast_to(scale_ref[pl.ds(t, 1), :], (8, LANES))
            for r in range(block // 16):
                piece = expo_ref[pl.ds(at + r * 16, 16), pl.ds(t * LANES, LANES)].astype(jnp.float32)
                acc[2 * r] += piece[:8] * scale
                acc[2 * r + 1] += piece[8:] * scale
        for r in range(block // 8):
            acc_ref[pl.ds(at + r * 8, 8), :] = acc[r]
        return 0

    lax.fori_loop(0, rows // block, body, 0)
    put_row_sums(acc_ref, out_ref, sums_ref)
    if extra_ref is not None and len(extra_ref.shape) == 3:
        for p in range(out_ref.shape[0]):
            out_ref[p, pl.ds(BLOCK, BLOCK), :] = extra_ref[0]
    elif extra_ref is not None:
        unit, unused_scale = unit_rows(extra_ref[...])
        unit = unit.astype(out_ref.dtype)
        share = unit.shape[0]
        for p in range(out_ref.shape[0]):
            out_ref[p, pl.ds(BLOCK, share), :] = unit[:, :LANES]
            out_ref[p, pl.ds(BLOCK + share, share), :] = unit[:, LANES:]


def col_kernel(expo_ref, got_ref, out_ref, scale_ref, sums_ref):
    rows, columns = expo_ref.shape
    scale = 1.0 / get_row_sums(got_ref, 0)
    for j in range(rows // LANES):
        scale_ref[pl.ds(j * LANES, LANES), :] = column_of(scale, j)
    tiles = 8

    for k in range(columns // (tiles * LANES)):

        def body(i, acc):
            acc = list(acc)
            at = pl.multiple_of(i * 64, 64)
            for r in range(4):
                weight = scale_ref[pl.ds(at + r * 16, 16), :]
                for t in range(tiles):
                    lanes = pl.ds((k * tiles + t) * LANES, LANES)
                    piece = expo_ref[pl.ds(at + r * 16, 16), lanes].astype(jnp.float32) * weight
                    acc[t] += piece[:8] + piece[8:]
            return tuple(acc)

        acc = lax.fori_loop(
            0, rows // 64, body, tuple(jnp.zeros((8, LANES), jnp.float32) for _ in range(tiles))
        )
        for t in range(tiles):
            sums_ref[pl.ds(k * tiles + t, 1), :] = jnp.sum(acc[t], axis=0, keepdims=True)
    sums = sums_ref[...].astype(out_ref.dtype)
    for p in range(out_ref.shape[0]):
        out_ref[p] = sums


def grad_kernel(
    core_ref, expo_ref, stud_ref, low_ref, wlow_ref, raw_ref, norm_ref, cols_ref, rows_ref,
    feat_far, keep_far, send_far, feat_ref, keep_ref, send_ref, out_sems,
    assign_ref, prob_ref, colscale_ref, acc_ref,
):
    rows, columns = expo_ref.shape
    factor = PROTOS / 32.0 / STUDENT_TEMP
    by_row = 1.0 / get_row_sums(rows_ref, 0)
    by_total = 1.0 / get_row_sums(rows_ref, BLOCK)
    colscale_ref[...] = 1.0 / jnp.sum(cols_ref[...].astype(jnp.float32), axis=0)
    for j in range(rows // LANES):
        at = pl.ds(j * LANES, LANES)
        assign_ref[at, :] = column_of(by_row, j) * factor
        prob_ref[at, :] = column_of(by_total, j) * factor
    core = core_ref[0]
    low = low_ref[...]
    stores = []
    for k in range(columns // WIDE):
        cols = pl.ds(k * WIDE, WIDE)
        pieces = []
        for t in range(WIDE // LANES):
            at = pl.ds(k * WIDE + t * LANES, LANES)
            scale = colscale_ref[pl.ds(k * (WIDE // LANES) + t, 1), :]
            pieces.append(
                (
                    stud_ref[:, at].astype(jnp.float32) * prob_ref[...]
                    - assign_ref[...] * (expo_ref[:, at].astype(jnp.float32) * scale)
                ).astype(jnp.bfloat16)
            )
        grad = jnp.concatenate(pieces, axis=1)
        feat = lax.dot_general(
            grad, wlow_ref[:, cols], (((1,), (1,)), ((), ())), preferred_element_type=jnp.float32
        )
        acc_ref[...] = feat if k == 0 else acc_ref[...] + feat
        proto = lax.dot_general(
            low, grad, (((0,), (0,)), ((), ())), preferred_element_type=jnp.float32
        )
        norm = norm_ref[:, cols]
        unit = raw_ref[:, cols].astype(jnp.float32) * norm
        dots = jnp.sum(unit * proto, axis=0, keepdims=True)
        part = norm * (proto - unit * dots)
        part = part.reshape(8, 2, 16, WIDE)
        slot = k % 2
        if k >= 2:
            for copy in stores[k - 2]:
                copy.wait()
        keep_ref[slot] = jnp.where(core == 0, part[:, 0], part[:, 1])
        send_ref[slot] = jnp.where(core == 0, part[:, 1], part[:, 0]).astype(jnp.bfloat16)
        stores.append(
            (
                pltpu.make_async_copy(
                    keep_ref.at[slot], keep_far.at[:, :, cols], out_sems.at[0, slot]
                ),
                pltpu.make_async_copy(
                    send_ref.at[slot], send_far.at[:, :, cols], out_sems.at[1, slot]
                ),
            )
        )
        for copy in stores[k]:
            copy.start()
    low = low.astype(jnp.float32)
    feat = acc_ref[...]
    inner = jnp.sum(low * feat, axis=1, keepdims=True)
    feat = (feat - low * inner).astype(jnp.bfloat16)
    count = feat_ref.shape[0]
    share = rows // count
    spot = diagonal(share, feat.shape[1])
    for p in range(count):
        mine = slice(p * share, (p + 1) * share)
        feat_ref[p, pl.ds(0, share), :] = feat[mine]
        along = jnp.sum(jnp.where(spot, inner[mine], 0.0), axis=0, keepdims=True)
        feat_ref[p, pl.ds(share, BLOCK), :] = jnp.broadcast_to(
            along, (BLOCK, feat.shape[1])
        ).astype(jnp.bfloat16)
    last = pltpu.make_async_copy(feat_ref, feat_far, out_sems.at[2, 0])
    last.start()
    for pair in stores[-2:]:
        for copy in pair:
            copy.wait()
    last.wait()


def exchange(copies, axis):
    return lax.all_to_all(copies, axis, 0, 0, tiled=True)


def spread_sum(parts, axis, dim, me, target, dtype=jnp.float32):
    total = lax.dynamic_index_in_dim(parts, me, dim, keepdims=False)
    for hop in (2, 1, 3):
        part = lax.dynamic_index_in_dim(parts, (me + hop) % 4, dim, keepdims=False).astype(dtype)
        got = lax.ppermute(part, axis, [(i, target(i, hop)) for i in range(16)])
        total = total + got.astype(jnp.float32)
    return total


def on_device(
    teacher_hidden,
    student_hidden,
    teacher_bottleneck,
    student_bottleneck,
    teacher_prototypes,
    student_prototypes,
):
    f32, bf16 = jnp.float32, jnp.bfloat16
    shape = jax.ShapeDtypeStruct
    rows = teacher_hidden.shape[0]
    columns = teacher_prototypes.shape[1]
    width = teacher_prototypes.shape[0]
    row_tiles, col_tiles = rows // LANES, columns // LANES
    n_dp, n_proto = lax.axis_size("dp"), lax.axis_size("proto")

    def blocks_of(part, count):
        return part.astype(bf16).reshape(count, part.shape[0] // count, part.shape[1])

    teach_part = jnp.dot(teacher_hidden, teacher_bottleneck, preferred_element_type=f32)
    got = exchange(blocks_of(teach_part, n_proto), "proto")

    me, where = lax.axis_index("proto"), lax.axis_index("dp")
    core, high, y_at = jnp.reshape(where % 2, (1,)), (where // 2) % 2, where // 4
    share = rows // n_proto
    teach_norm = col_scales(teacher_prototypes)
    stud_norm = col_scales(student_prototypes)
    teach_norm, stud_norm, stud_early = lax.optimization_barrier(
        (teach_norm, stud_norm, student_hidden)
    )
    stud_part = jnp.dot(stud_early, student_bottleneck, preferred_element_type=f32)
    stud_part = stud_part.reshape(4, 4, share, width)
    stud_line = spread_sum(stud_part, "proto", 1, me % 4, lambda i, hop: i // 4 * 4 + (i + hop) % 4)

    (copies,) = on_core(share_kernel, [shape(got.shape, bf16)], (got,))
    copies, teach_norm, stud_norm = lax.optimization_barrier((copies, teach_norm, stud_norm))
    teach_low = exchange(copies, "proto").reshape(rows, width)
    teach_wlow = (teacher_prototypes.astype(f32) * teach_norm).astype(bf16)
    teach_wlow, stud_line, stud_norm = lax.optimization_barrier((teach_wlow, stud_line, stud_norm))
    stud_wlow = (student_prototypes.astype(f32) * stud_norm).astype(bf16)
    stud_share = spread_sum(stud_line, "proto", 0, me // 4, lambda i, hop: (i + 4 * hop) % 16)

    teach_low, teach_wlow, stud_norm, stud_wlow, stud_share, core, high, y_at = (
        lax.optimization_barrier(
            (teach_low, teach_wlow, stud_norm, stud_wlow, stud_share, core, high, y_at)
        )
    )

    big = pltpu.VMEM((rows, columns), KEEP)
    chunks = columns // WIDE
    weights = [pltpu.VMEM((width, columns), bf16), pltpu.SemaphoreType.DMA((chunks,))]
    row_acc = [pltpu.VMEM((rows, LANES), f32), pltpu.VMEM((8, LANES), f32)]
    col_sums = pltpu.VMEM((col_tiles, LANES), f32)
    expo, copies = on_core(
        teacher_kernel,
        [big, shape((n_dp, col_tiles, LANES), bf16)],
        (teach_low, teach_wlow),
        scratch=weights + [col_sums],
        far=(1,),
    )
    for step in range(ITERS):
        got_cols = exchange(copies, "dp")
        count, extra = BLOCK, ()
        if step == ITERS - 2:
            count, extra = BLOCK + 2 * share, (stud_share,)
        if step == ITERS - 1:
            got_rows, got_cols = lax.optimization_barrier((got_rows, got_cols))
            stud_expo, totals, stud_low = on_core(
                student_kernel,
                [
                    pltpu.VMEM((rows, columns), bf16),
                    shape((1, BLOCK, LANES), bf16),
                    shape((rows, width), bf16),
                ],
                (got_rows, stud_wlow),
                scratch=row_acc,
            )
            count, extra = 2 * BLOCK, (totals,)
        (copies,) = on_core(
            row_kernel,
            [shape((n_proto, count, LANES), bf16)],
            (expo, got_cols) + extra,
            scratch=[col_sums] + row_acc,
            pinned=(0,),
        )
        got_rows = exchange(copies, "proto")
        if step < ITERS - 1:
            (copies,) = on_core(
                col_kernel,
                [shape((n_dp, col_tiles, LANES), bf16)],
                (expo, got_rows),
                scratch=[pltpu.VMEM((rows, LANES), f32), col_sums],
                pinned=(0,),
            )

    feat_part, keep, send = on_core(
        grad_kernel,
        [
            pltpu.HBM((n_proto, share + BLOCK, width), bf16),
            pltpu.HBM((8, 16, columns), f32),
            pltpu.HBM((8, 16, columns), bf16),
        ],
        (
            core, expo, stud_expo, stud_low, stud_wlow,
            student_prototypes, stud_norm, got_cols, got_rows,
        ),
        scratch=[
            pltpu.VMEM((n_proto, share + BLOCK, width), bf16),
            pltpu.VMEM((2, 8, 16, WIDE), f32),
            pltpu.VMEM((2, 8, 16, WIDE), bf16),
            pltpu.SemaphoreType.DMA((3, 2)),
            pltpu.VMEM((rows, LANES), f32),
            pltpu.VMEM((rows, LANES), f32),
            pltpu.VMEM((col_tiles, LANES), f32),
            pltpu.VMEM((rows, width), f32),
        ],
        pinned=(1, 2),
        smem=(0,),
        far_outs=(0, 1, 2),
    )

    got = exchange(feat_part, "proto")
    (copies,) = on_core(proj_kernel, [shape((n_proto, share, width), bf16)], (got, stud_share))
    proj_grad = exchange(copies, "proto").reshape(rows, width)
    bottle_part = lax.dot_general(
        proj_grad, student_hidden, (((0,), (0,)), ((), ())), preferred_element_type=f32
    )
    got_bottle = exchange(blocks_of(bottle_part, n_dp), "dp")
    grad_bottleneck = jnp.sum(got_bottle.astype(f32), axis=0).T

    got = lax.ppermute(send, "dp", [(i, i ^ 1) for i in range(16)])
    pair = (keep + got.astype(f32)).reshape(4, 2, 16, columns)
    quarter = spread_sum(pair, "dp", 0, y_at, lambda i, hop: (i + 4 * hop) % 16, bf16)
    keep = jnp.where(high == 0, quarter[0], quarter[1])
    send = jnp.where(high == 0, quarter[1], quarter[0]).astype(bf16)
    got = lax.ppermute(send, "dp", [(i, i ^ 2) for i in range(16)])
    grad_prototypes = keep + got.astype(f32)
    return (grad_prototypes, grad_bottleneck)


def solution(mesh):
    return jax.shard_map(
        on_device,
        mesh=mesh,
        in_specs=(
            P("dp", "proto"),
            P("dp", "proto"),
            P("proto", None),
            P("proto", None),
            P(None, "proto"),
            P(None, "proto"),
        ),
        out_specs=(P("dp", "proto"), P("proto", "dp")),
        check_vma=False,
    )
```

```python
import jax
import jax.numpy as jnp
from jax import lax
from jax.experimental import pallas as pl
from jax.experimental.pallas import tpu as pltpu
from jax.sharding import PartitionSpec as P

PROTOS = 65536
ITERS = 3

TEACHER_TEMP = 0.07
STUDENT_TEMP = 0.1
EPSILON = 1e-06
LOG2E = 1.4426950408889634

LANES = 128
WIDE = 512
LIMIT = 16 * 2**20
KEEP = jnp.float32
BLOCK = 16


def unit_rows(values):
    scale = lax.rsqrt(jnp.sum(values * values, axis=1, keepdims=True) + EPSILON)
    return (values * scale, scale)


def col_scales(weights):
    values = weights.astype(jnp.float32)
    return lax.rsqrt(jnp.sum(values * values, axis=0, keepdims=True) + EPSILON)


def on_core(kernel, outs, args, scratch=(), pinned=(), smem=(), far=(), far_outs=()):
    args = [
        pltpu.with_memory_space_constraint(a, pltpu.VMEM if i in pinned else pltpu.HBM)
        if i in pinned or i in far
        else a
        for i, a in enumerate(args)
    ]

    def place(i, far_ones):
        return pl.BlockSpec(memory_space=pltpu.HBM if i in far_ones else pltpu.VMEM)

    return pl.pallas_call(
        kernel,
        out_shape=tuple(outs),
        in_specs=[
            pl.BlockSpec(memory_space=pltpu.SMEM) if i in smem else place(i, far)
            for i in range(len(args))
        ],
        out_specs=tuple(place(i, far_outs) for i in range(len(outs))),
        scratch_shapes=list(scratch),
        compiler_params=pltpu.CompilerParams(vmem_limit_bytes=LIMIT),
    )(*args)


def column_of(rows, j):
    return jnp.broadcast_to(rows[j : j + 1, :], (LANES, LANES)).T


def put_row_sums(acc_ref, out_ref, sums_ref):
    sums_ref[...] = jnp.zeros_like(sums_ref)
    for j in range(acc_ref.shape[0] // LANES):
        sums_ref[pl.ds(j, 1), :] = jnp.sum(
            acc_ref[pl.ds(j * LANES, LANES), :].T, axis=0, keepdims=True
        )
    sums = sums_ref[...]
    high = sums.astype(jnp.bfloat16).astype(jnp.float32)
    block = jnp.concatenate([high, sums - high], axis=0).astype(jnp.bfloat16)
    for p in range(out_ref.shape[0]):
        out_ref[p, pl.ds(0, BLOCK), :] = block


def get_row_sums(got_ref, first):
    terms = jnp.sum(got_ref[:, pl.ds(first, BLOCK), :].astype(jnp.float32), axis=0)
    return terms[:8] + terms[8:]


def diagonal(rows, columns):
    shape = (rows, columns)
    return lax.broadcasted_iota(jnp.int32, shape, 0) == lax.broadcasted_iota(jnp.int32, shape, 1)


def share_kernel(got_ref, out_ref):
    unit, unused_scale = unit_rows(jnp.sum(got_ref[...].astype(jnp.float32), axis=0))
    unit = unit.astype(out_ref.dtype)
    for p in range(out_ref.shape[0]):
        out_ref[p] = unit


def proj_kernel(got_ref, share_ref, out_ref):
    unit, scale = unit_rows(share_ref[...])
    share, width = unit.shape
    got = jnp.sum(got_ref[...].astype(jnp.float32), axis=0)
    along = jnp.where(diagonal(share, width), got[share : share + 1], 0.0)
    low = unit.astype(jnp.bfloat16).astype(jnp.float32)
    feat = got[:share] + low * jnp.sum(along, axis=1, keepdims=True)
    inner = jnp.sum(unit * feat, axis=1, keepdims=True)
    rows = (scale * (feat - unit * inner)).astype(out_ref.dtype)
    for p in range(out_ref.shape[0]):
        out_ref[p] = rows


def teacher_kernel(low_ref, w_ref, expo_ref, out_ref, sums_ref):
    low = low_ref[...]
    for k in range(w_ref.shape[1] // WIDE):
        cols = pl.ds(k * WIDE, WIDE)
        scores = jnp.dot(low, w_ref[:, cols], preferred_element_type=jnp.float32)
        expo = jnp.exp2(scores * (LOG2E / TEACHER_TEMP))
        expo_ref[:, cols] = expo.astype(expo_ref.dtype)
        sums = jnp.sum(expo, axis=0, keepdims=True)
        for t in range(WIDE // LANES):
            sums_ref[pl.ds(k * (WIDE // LANES) + t, 1), :] = sums[:, t * LANES : (t + 1) * LANES]
    sums = sums_ref[...].astype(out_ref.dtype)
    for p in range(out_ref.shape[0]):
        out_ref[p] = sums


def student_kernel(got_ref, w_ref, expo_ref, totals_ref, low_ref, acc_ref, sums_ref):
    share = (got_ref.shape[1] - BLOCK) // 2
    for p in range(got_ref.shape[0]):
        for half in range(2):
            low_ref[pl.ds(p * share, share), pl.ds(half * LANES, LANES)] = got_ref[
                p, pl.ds(BLOCK + half * share, share), :
            ]
    low = low_ref[...]
    for k in range(w_ref.shape[1] // WIDE):
        cols = pl.ds(k * WIDE, WIDE)
        scores = jnp.dot(low, w_ref[:, cols], preferred_element_type=jnp.float32)
        expo = jnp.exp2(scores * (LOG2E / STUDENT_TEMP))
        expo_ref[:, cols] = expo.astype(expo_ref.dtype)
        part = sum(expo[:, t * LANES : (t + 1) * LANES] for t in range(WIDE // LANES))
        acc_ref[...] = part if k == 0 else acc_ref[...] + part
    put_row_sums(acc_ref, totals_ref, sums_ref)


def row_kernel(expo_ref, got_ref, *refs):
    extra_ref = refs[0] if len(refs) == 5 else None
    out_ref, scale_ref, acc_ref, sums_ref = refs[-4:]
    rows, columns = expo_ref.shape
    scale_ref[...] = 1.0 / jnp.sum(got_ref[...].astype(jnp.float32), axis=0)
    block = 64

    def body(i, _):
        at = pl.multiple_of(i * block, block)
        acc = [jnp.zeros((8, LANES), jnp.float32)] * (block // 8)
        for t in range(columns // LANES):
            scale = jnp.broadcast_to(scale_ref[pl.ds(t, 1), :], (8, LANES))
            for r in range(block // 16):
                piece = expo_ref[pl.ds(at + r * 16, 16), pl.ds(t * LANES, LANES)].astype(jnp.float32)
                acc[2 * r] += piece[:8] * scale
                acc[2 * r + 1] += piece[8:] * scale
        for r in range(block // 8):
            acc_ref[pl.ds(at + r * 8, 8), :] = acc[r]
        return 0

    lax.fori_loop(0, rows // block, body, 0)
    put_row_sums(acc_ref, out_ref, sums_ref)
    if extra_ref is not None and len(extra_ref.shape) == 3:
        for p in range(out_ref.shape[0]):
            out_ref[p, pl.ds(BLOCK, BLOCK), :] = extra_ref[0]
    elif extra_ref is not None:
        unit, unused_scale = unit_rows(extra_ref[...])
        unit = unit.astype(out_ref.dtype)
        share = unit.shape[0]
        for p in range(out_ref.shape[0]):
            out_ref[p, pl.ds(BLOCK, share), :] = unit[:, :LANES]
            out_ref[p, pl.ds(BLOCK + share, share), :] = unit[:, LANES:]


def col_kernel(expo_ref, got_ref, out_ref, scale_ref, sums_ref):
    rows, columns = expo_ref.shape
    scale = 1.0 / get_row_sums(got_ref, 0)
    for j in range(rows // LANES):
        scale_ref[pl.ds(j * LANES, LANES), :] = column_of(scale, j)
    tiles = 8

    for k in range(columns // (tiles * LANES)):

        def body(i, acc):
            acc = list(acc)
            at = pl.multiple_of(i * 64, 64)
            for r in range(4):
                weight = scale_ref[pl.ds(at + r * 16, 16), :]
                for t in range(tiles):
                    lanes = pl.ds((k * tiles + t) * LANES, LANES)
                    piece = expo_ref[pl.ds(at + r * 16, 16), lanes].astype(jnp.float32) * weight
                    acc[t] += piece[:8] + piece[8:]
            return tuple(acc)

        acc = lax.fori_loop(
            0, rows // 64, body, tuple(jnp.zeros((8, LANES), jnp.float32) for _ in range(tiles))
        )
        for t in range(tiles):
            sums_ref[pl.ds(k * tiles + t, 1), :] = jnp.sum(acc[t], axis=0, keepdims=True)
    sums = sums_ref[...].astype(out_ref.dtype)
    for p in range(out_ref.shape[0]):
        out_ref[p] = sums


def grad_kernel(
    core_ref, expo_ref, stud_ref, low_ref, wlow_ref, raw_ref, norm_ref, cols_ref, rows_ref,
    feat_far, keep_far, send_far, feat_ref, keep_ref, send_ref, out_sems,
    assign_ref, prob_ref, colscale_ref, acc_ref,
):
    rows, columns = expo_ref.shape
    factor = PROTOS / 32.0 / STUDENT_TEMP
    by_row = 1.0 / get_row_sums(rows_ref, 0)
    by_total = 1.0 / get_row_sums(rows_ref, BLOCK)
    colscale_ref[...] = 1.0 / jnp.sum(cols_ref[...].astype(jnp.float32), axis=0)
    for j in range(rows // LANES):
        at = pl.ds(j * LANES, LANES)
        assign_ref[at, :] = column_of(by_row, j) * factor
        prob_ref[at, :] = column_of(by_total, j) * factor
    core = core_ref[0]
    low = low_ref[...]
    stores = []
    for k in range(columns // WIDE):
        cols = pl.ds(k * WIDE, WIDE)
        pieces = []
        for t in range(WIDE // LANES):
            at = pl.ds(k * WIDE + t * LANES, LANES)
            scale = colscale_ref[pl.ds(k * (WIDE // LANES) + t, 1), :]
            pieces.append(
                (
                    stud_ref[:, at].astype(jnp.float32) * prob_ref[...]
                    - assign_ref[...] * (expo_ref[:, at].astype(jnp.float32) * scale)
                ).astype(jnp.bfloat16)
            )
        grad = jnp.concatenate(pieces, axis=1)
        feat = lax.dot_general(
            grad, wlow_ref[:, cols], (((1,), (1,)), ((), ())), preferred_element_type=jnp.float32
        )
        acc_ref[...] = feat if k == 0 else acc_ref[...] + feat
        proto = lax.dot_general(
            low, grad, (((0,), (0,)), ((), ())), preferred_element_type=jnp.float32
        )
        norm = norm_ref[:, cols]
        unit = raw_ref[:, cols].astype(jnp.float32) * norm
        dots = jnp.sum(unit * proto, axis=0, keepdims=True)
        part = norm * (proto - unit * dots)
        part = part.reshape(8, 2, 16, WIDE)
        slot = k % 2
        if k >= 2:
            for copy in stores[k - 2]:
                copy.wait()
        keep_ref[slot] = jnp.where(core == 0, part[:, 0], part[:, 1])
        send_ref[slot] = jnp.where(core == 0, part[:, 1], part[:, 0]).astype(jnp.bfloat16)
        stores.append(
            (
                pltpu.make_async_copy(
                    keep_ref.at[slot], keep_far.at[:, :, cols], out_sems.at[0, slot]
                ),
                pltpu.make_async_copy(
                    send_ref.at[slot], send_far.at[:, :, cols], out_sems.at[1, slot]
                ),
            )
        )
        for copy in stores[k]:
            copy.start()
    low = low.astype(jnp.float32)
    feat = acc_ref[...]
    inner = jnp.sum(low * feat, axis=1, keepdims=True)
    feat = (feat - low * inner).astype(jnp.bfloat16)
    count = feat_ref.shape[0]
    share = rows // count
    spot = diagonal(share, feat.shape[1])
    for p in range(count):
        mine = slice(p * share, (p + 1) * share)
        feat_ref[p, pl.ds(0, share), :] = feat[mine]
        along = jnp.sum(jnp.where(spot, inner[mine], 0.0), axis=0, keepdims=True)
        feat_ref[p, pl.ds(share, BLOCK), :] = jnp.broadcast_to(
            along, (BLOCK, feat.shape[1])
        ).astype(jnp.bfloat16)
    last = pltpu.make_async_copy(feat_ref, feat_far, out_sems.at[2, 0])
    last.start()
    for pair in stores[-2:]:
        for copy in pair:
            copy.wait()
    last.wait()


def exchange(copies, axis):
    return lax.all_to_all(copies, axis, 0, 0, tiled=True)


def spread_sum(parts, axis, dim, me, target, dtype=jnp.float32):
    total = lax.dynamic_index_in_dim(parts, me, dim, keepdims=False)
    for hop in (2, 1, 3):
        part = lax.dynamic_index_in_dim(parts, (me + hop) % 4, dim, keepdims=False).astype(dtype)
        got = lax.ppermute(part, axis, [(i, target(i, hop)) for i in range(16)])
        total = total + got.astype(jnp.float32)
    return total


def on_device(
    teacher_hidden,
    student_hidden,
    teacher_bottleneck,
    student_bottleneck,
    teacher_prototypes,
    student_prototypes,
):
    f32, bf16 = jnp.float32, jnp.bfloat16
    shape = jax.ShapeDtypeStruct
    rows = teacher_hidden.shape[0]
    columns = teacher_prototypes.shape[1]
    width = teacher_prototypes.shape[0]
    row_tiles, col_tiles = rows // LANES, columns // LANES
    n_dp, n_proto = lax.axis_size("dp"), lax.axis_size("proto")

    def blocks_of(part, count):
        return part.astype(bf16).reshape(count, part.shape[0] // count, part.shape[1])

    teach_part = jnp.dot(teacher_hidden, teacher_bottleneck, preferred_element_type=f32)
    got = exchange(blocks_of(teach_part, n_proto), "proto")

    me, where = lax.axis_index("proto"), lax.axis_index("dp")
    core, high, y_at = jnp.reshape(where % 2, (1,)), (where // 2) % 2, where // 4
    share = rows // n_proto
    teach_norm = col_scales(teacher_prototypes)
    stud_norm = col_scales(student_prototypes)
    stud_part = jnp.dot(student_hidden, student_bottleneck, preferred_element_type=f32)
    stud_part = stud_part.reshape(4, 4, share, width)
    stud_line = spread_sum(stud_part, "proto", 1, me % 4, lambda i, hop: i // 4 * 4 + (i + hop) % 4)

    (copies,) = on_core(share_kernel, [shape(got.shape, bf16)], (got,))
    copies, teach_norm, stud_norm, stud_line = lax.optimization_barrier(
        (copies, teach_norm, stud_norm, stud_line)
    )
    teach_low = exchange(copies, "proto").reshape(rows, width)
    teach_wlow = (teacher_prototypes.astype(f32) * teach_norm).astype(bf16)
    stud_wlow = (student_prototypes.astype(f32) * stud_norm).astype(bf16)
    teach_wlow, stud_wlow, stud_line = lax.optimization_barrier((teach_wlow, stud_wlow, stud_line))
    stud_share = spread_sum(stud_line, "proto", 0, me // 4, lambda i, hop: (i + 4 * hop) % 16)

    teach_low, teach_wlow, stud_norm, stud_wlow, stud_share, core, high, y_at = (
        lax.optimization_barrier(
            (teach_low, teach_wlow, stud_norm, stud_wlow, stud_share, core, high, y_at)
        )
    )

    big = pltpu.VMEM((rows, columns), KEEP)
    row_acc = [pltpu.VMEM((rows, LANES), f32), pltpu.VMEM((8, LANES), f32)]
    col_sums = pltpu.VMEM((col_tiles, LANES), f32)
    expo, copies = on_core(
        teacher_kernel,
        [big, shape((n_dp, col_tiles, LANES), bf16)],
        (teach_low, teach_wlow),
        scratch=[col_sums],
    )
    for step in range(ITERS):
        got_cols = exchange(copies, "dp")
        count, extra = BLOCK, ()
        if step == ITERS - 2:
            count, extra = BLOCK + 2 * share, (stud_share,)
        if step == ITERS - 1:
            got_rows, got_cols = lax.optimization_barrier((got_rows, got_cols))
            stud_expo, totals, stud_low = on_core(
                student_kernel,
                [
                    pltpu.VMEM((rows, columns), bf16),
                    shape((1, BLOCK, LANES), bf16),
                    shape((rows, width), bf16),
                ],
                (got_rows, stud_wlow),
                scratch=row_acc,
            )
            count, extra = 2 * BLOCK, (totals,)
        (copies,) = on_core(
            row_kernel,
            [shape((n_proto, count, LANES), bf16)],
            (expo, got_cols) + extra,
            scratch=[col_sums] + row_acc,
            pinned=(0,),
        )
        got_rows = exchange(copies, "proto")
        if step < ITERS - 1:
            (copies,) = on_core(
                col_kernel,
                [shape((n_dp, col_tiles, LANES), bf16)],
                (expo, got_rows),
                scratch=[pltpu.VMEM((rows, LANES), f32), col_sums],
                pinned=(0,),
            )

    feat_part, keep, send = on_core(
        grad_kernel,
        [
            pltpu.HBM((n_proto, share + BLOCK, width), bf16),
            pltpu.HBM((8, 16, columns), f32),
            pltpu.HBM((8, 16, columns), bf16),
        ],
        (
            core, expo, stud_expo, stud_low, stud_wlow,
            student_prototypes, stud_norm, got_cols, got_rows,
        ),
        scratch=[
            pltpu.VMEM((n_proto, share + BLOCK, width), bf16),
            pltpu.VMEM((2, 8, 16, WIDE), f32),
            pltpu.VMEM((2, 8, 16, WIDE), bf16),
            pltpu.SemaphoreType.DMA((3, 2)),
            pltpu.VMEM((rows, LANES), f32),
            pltpu.VMEM((rows, LANES), f32),
            pltpu.VMEM((col_tiles, LANES), f32),
            pltpu.VMEM((rows, width), f32),
        ],
        pinned=(1, 2),
        smem=(0,),
        far_outs=(0, 1, 2),
    )

    got = exchange(feat_part, "proto")
    (copies,) = on_core(proj_kernel, [shape((n_proto, share, width), bf16)], (got, stud_share))
    proj_grad = exchange(copies, "proto").reshape(rows, width)
    got = lax.ppermute(send, "dp", [(i, i ^ 1) for i in range(16)])
    pair = (keep + got.astype(f32)).reshape(4, 2, 16, columns)
    quarter = spread_sum(pair, "dp", 0, y_at, lambda i, hop: (i + 4 * hop) % 16, bf16)
    proj_grad, quarter = lax.optimization_barrier((proj_grad, quarter))
    keep = jnp.where(high == 0, quarter[0], quarter[1])
    send = jnp.where(high == 0, quarter[1], quarter[0]).astype(bf16)
    got = lax.ppermute(send, "dp", [(i, i ^ 2) for i in range(16)])
    grad_prototypes = keep + got.astype(f32)
    bottle_part = lax.dot_general(
        proj_grad, student_hidden, (((0,), (0,)), ((), ())), preferred_element_type=f32
    )
    got_bottle = exchange(blocks_of(bottle_part, n_dp), "dp")
    grad_bottleneck = jnp.sum(got_bottle.astype(f32), axis=0).T

    return (grad_prototypes, grad_bottleneck)


def solution(mesh):
    return jax.shard_map(
        on_device,
        mesh=mesh,
        in_specs=(
            P("dp", "proto"),
            P("dp", "proto"),
            P("proto", None),
            P("proto", None),
            P(None, "proto"),
            P(None, "proto"),
        ),
        out_specs=(P("dp", "proto"), P("proto", "dp")),
        check_vma=False,
    )
```

```python
import jax
import jax.numpy as jnp
from jax import lax
from jax.experimental import pallas as pl
from jax.experimental.pallas import tpu as pltpu
from jax.sharding import PartitionSpec as P

PROTOS = 65536
ITERS = 3

TEACHER_TEMP = 0.07
STUDENT_TEMP = 0.1
EPSILON = 1e-06
LOG2E = 1.4426950408889634

LANES = 128
WIDE = 512
GRAD_WIDE = 1024
LIMIT = 16 * 2**20
KEEP = jnp.float32
HOPS = (2, 1, 3)
BLOCK = 16


def unit_rows(values):
    scale = lax.rsqrt(jnp.sum(values * values, axis=1, keepdims=True) + EPSILON)
    return (values * scale, scale)


def col_scales(weights):
    values = weights.astype(jnp.float32)
    return lax.rsqrt(jnp.sum(values * values, axis=0, keepdims=True) + EPSILON)


def on_core(kernel, outs, args, scratch=(), pinned=(), smem=(), far=(), far_outs=()):
    args = [
        pltpu.with_memory_space_constraint(a, pltpu.VMEM if i in pinned else pltpu.HBM)
        if i in pinned or i in far
        else a
        for i, a in enumerate(args)
    ]

    def place(i, far_ones):
        return pl.BlockSpec(memory_space=pltpu.HBM if i in far_ones else pltpu.VMEM)

    return pl.pallas_call(
        kernel,
        out_shape=tuple(outs),
        in_specs=[
            pl.BlockSpec(memory_space=pltpu.SMEM) if i in smem else place(i, far)
            for i in range(len(args))
        ],
        out_specs=tuple(place(i, far_outs) for i in range(len(outs))),
        scratch_shapes=list(scratch),
        compiler_params=pltpu.CompilerParams(vmem_limit_bytes=LIMIT),
    )(*args)


def column_of(rows, j):
    return jnp.broadcast_to(rows[j : j + 1, :], (LANES, LANES)).T


def put_row_sums(acc_ref, out_ref, sums_ref):
    sums_ref[...] = jnp.zeros_like(sums_ref)
    for j in range(acc_ref.shape[0] // LANES):
        sums_ref[pl.ds(j, 1), :] = jnp.sum(
            acc_ref[pl.ds(j * LANES, LANES), :].T, axis=0, keepdims=True
        )
    sums = sums_ref[...]
    high = sums.astype(jnp.bfloat16).astype(jnp.float32)
    block = jnp.concatenate([high, sums - high], axis=0).astype(jnp.bfloat16)
    for p in range(out_ref.shape[0]):
        out_ref[p, pl.ds(0, BLOCK), :] = block


def get_row_sums(got_ref, first):
    terms = jnp.sum(got_ref[:, pl.ds(first, BLOCK), :].astype(jnp.float32), axis=0)
    return terms[:8] + terms[8:]


def diagonal(rows, columns):
    shape = (rows, columns)
    return lax.broadcasted_iota(jnp.int32, shape, 0) == lax.broadcasted_iota(jnp.int32, shape, 1)


def share_kernel(got_ref, out_ref):
    unit, unused_scale = unit_rows(jnp.sum(got_ref[...].astype(jnp.float32), axis=0))
    unit = unit.astype(out_ref.dtype)
    for p in range(out_ref.shape[0]):
        out_ref[p] = unit


def parts_kernel(at_ref, hidden_ref, weight_ref, *refs):
    part_ref = refs[-1]
    count, share, width = part_ref.shape
    part = jnp.dot(hidden_ref[...], weight_ref[...], preferred_element_type=jnp.float32)
    part_ref[...] = part.reshape(count, share, width)
    for out_ref, hop in zip(refs[:-1], (0,) + HOPS):
        for line in range(4):
            out_ref[line] = part_ref[line * 4 + ((at_ref[0] + hop) & 3)]


def line_kernel(at_ref, own_ref, one_ref, two_ref, three_ref, unused_ref, *refs):
    sum_ref = refs[-1]
    sum_ref[...] = own_ref[...] + one_ref[...] + two_ref[...] + three_ref[...]
    for out_ref, hop in zip(refs[:-1], (0,) + HOPS):
        out_ref[...] = sum_ref[(at_ref[0] + hop) & 3]


def proj_kernel(got_ref, share_ref, out_ref):
    unit, scale = unit_rows(share_ref[...])
    share = unit.shape[0]
    got = jnp.sum(got_ref[...].astype(jnp.float32), axis=0)
    along = jnp.where(diagonal(share, LANES), got[2 * share : 2 * share + 1], 0.0)
    low = unit.astype(jnp.bfloat16).astype(jnp.float32)
    feat = jnp.concatenate([got[:share], got[share : 2 * share]], axis=1)
    feat = feat + low * jnp.sum(along, axis=1, keepdims=True)
    inner = jnp.sum(unit * feat, axis=1, keepdims=True)
    rows = (scale * (feat - unit * inner)).astype(out_ref.dtype)
    for p in range(out_ref.shape[0]):
        out_ref[p] = rows


def teacher_kernel(low_ref, w_ref, expo_ref, out_ref, sums_ref):
    low = low_ref[...]
    for k in range(w_ref.shape[1] // WIDE):
        cols = pl.ds(k * WIDE, WIDE)
        scores = jnp.dot(low, w_ref[:, cols], preferred_element_type=jnp.float32)
        expo = jnp.exp2(scores * (LOG2E / TEACHER_TEMP))
        expo_ref[:, cols] = expo.astype(expo_ref.dtype)
        sums = jnp.sum(expo, axis=0, keepdims=True)
        for t in range(WIDE // LANES):
            sums_ref[pl.ds(k * (WIDE // LANES) + t, 1), :] = sums[:, t * LANES : (t + 1) * LANES]
    sums = sums_ref[...].astype(out_ref.dtype)
    for p in range(out_ref.shape[0]):
        out_ref[p] = sums


def student_kernel(got_ref, w_ref, expo_ref, totals_ref, low_ref, acc_ref, sums_ref):
    share = (got_ref.shape[1] - BLOCK) // 2
    for p in range(got_ref.shape[0]):
        for half in range(2):
            low_ref[pl.ds(p * share, share), pl.ds(half * LANES, LANES)] = got_ref[
                p, pl.ds(BLOCK + half * share, share), :
            ]
    low = low_ref[...]
    for k in range(w_ref.shape[1] // WIDE):
        cols = pl.ds(k * WIDE, WIDE)
        scores = jnp.dot(low, w_ref[:, cols], preferred_element_type=jnp.float32)
        expo = jnp.exp2(scores * (LOG2E / STUDENT_TEMP))
        expo_ref[:, cols] = expo.astype(expo_ref.dtype)
        part = sum(expo[:, t * LANES : (t + 1) * LANES] for t in range(WIDE // LANES))
        acc_ref[...] = part if k == 0 else acc_ref[...] + part
    put_row_sums(acc_ref, totals_ref, sums_ref)


def row_kernel(expo_ref, got_ref, *refs):
    extra_ref = refs[0] if len(refs) == 5 else None
    out_ref, scale_ref, acc_ref, sums_ref = refs[-4:]
    rows, columns = expo_ref.shape
    scale_ref[...] = 1.0 / jnp.sum(got_ref[...].astype(jnp.float32), axis=0)
    block = 64

    def body(i, _):
        at = pl.multiple_of(i * block, block)
        acc = [jnp.zeros((8, LANES), jnp.float32)] * (block // 8)
        for t in range(columns // LANES):
            scale = jnp.broadcast_to(scale_ref[pl.ds(t, 1), :], (8, LANES))
            for r in range(block // 16):
                piece = expo_ref[pl.ds(at + r * 16, 16), pl.ds(t * LANES, LANES)].astype(jnp.float32)
                acc[2 * r] += piece[:8] * scale
                acc[2 * r + 1] += piece[8:] * scale
        for r in range(block // 8):
            acc_ref[pl.ds(at + r * 8, 8), :] = acc[r]
        return 0

    lax.fori_loop(0, rows // block, body, 0)
    put_row_sums(acc_ref, out_ref, sums_ref)
    if extra_ref is not None and len(extra_ref.shape) == 3:
        for p in range(out_ref.shape[0]):
            out_ref[p, pl.ds(BLOCK, BLOCK), :] = extra_ref[0]
    elif extra_ref is not None:
        unit, unused_scale = unit_rows(extra_ref[...])
        unit = unit.astype(out_ref.dtype)
        share = unit.shape[0]
        for p in range(out_ref.shape[0]):
            out_ref[p, pl.ds(BLOCK, share), :] = unit[:, :LANES]
            out_ref[p, pl.ds(BLOCK + share, share), :] = unit[:, LANES:]


def col_kernel(expo_ref, got_ref, out_ref, scale_ref, sums_ref):
    rows, columns = expo_ref.shape
    scale = 1.0 / get_row_sums(got_ref, 0)
    for j in range(rows // LANES):
        scale_ref[pl.ds(j * LANES, LANES), :] = column_of(scale, j)
    tiles = 8

    for k in range(columns // (tiles * LANES)):

        def body(i, acc):
            acc = list(acc)
            at = pl.multiple_of(i * 64, 64)
            for r in range(4):
                weight = scale_ref[pl.ds(at + r * 16, 16), :]
                for t in range(tiles):
                    lanes = pl.ds((k * tiles + t) * LANES, LANES)
                    piece = expo_ref[pl.ds(at + r * 16, 16), lanes].astype(jnp.float32) * weight
                    acc[t] += piece[:8] + piece[8:]
            return tuple(acc)

        acc = lax.fori_loop(
            0, rows // 64, body, tuple(jnp.zeros((8, LANES), jnp.float32) for _ in range(tiles))
        )
        for t in range(tiles):
            sums_ref[pl.ds(k * tiles + t, 1), :] = jnp.sum(acc[t], axis=0, keepdims=True)
    sums = sums_ref[...].astype(out_ref.dtype)
    for p in range(out_ref.shape[0]):
        out_ref[p] = sums


def grad_kernel(
    core_ref, expo_ref, stud_ref, low_ref, wlow_ref, raw_ref, norm_ref, cols_ref, rows_ref,
    feat_far, keep_far, send_far, feat_ref, keep_ref, send_ref, out_sems,
    assign_ref, prob_ref, colscale_ref, acc_ref,
):
    rows, columns = expo_ref.shape
    factor = PROTOS / 32.0 / STUDENT_TEMP
    by_row = 1.0 / get_row_sums(rows_ref, 0)
    by_total = 1.0 / get_row_sums(rows_ref, BLOCK)
    colscale_ref[...] = 1.0 / jnp.sum(cols_ref[...].astype(jnp.float32), axis=0)
    for j in range(rows // LANES):
        at = pl.ds(j * LANES, LANES)
        assign_ref[at, :] = column_of(by_row, j) * factor
        prob_ref[at, :] = column_of(by_total, j) * factor
    core = core_ref[0]
    low = low_ref[...]
    stores = []
    for k in range(columns // GRAD_WIDE):
        cols = pl.ds(k * GRAD_WIDE, GRAD_WIDE)
        pieces = []
        for t in range(GRAD_WIDE // LANES):
            at = pl.ds(k * GRAD_WIDE + t * LANES, LANES)
            scale = colscale_ref[pl.ds(k * (GRAD_WIDE // LANES) + t, 1), :]
            pieces.append(
                (
                    stud_ref[:, at].astype(jnp.float32) * prob_ref[...]
                    - assign_ref[...] * (expo_ref[:, at].astype(jnp.float32) * scale)
                ).astype(jnp.bfloat16)
            )
        grad = jnp.concatenate(pieces, axis=1)
        feat = lax.dot_general(
            grad, wlow_ref[:, cols], (((1,), (1,)), ((), ())), preferred_element_type=jnp.float32
        )
        acc_ref[...] = feat if k == 0 else acc_ref[...] + feat
        proto = lax.dot_general(
            low, grad, (((0,), (0,)), ((), ())), preferred_element_type=jnp.float32
        )
        norm = norm_ref[:, cols]
        unit = raw_ref[:, cols].astype(jnp.float32) * norm
        dots = jnp.sum(unit * proto, axis=0, keepdims=True)
        part = norm * (proto - unit * dots)
        part = part.reshape(8, 2, 16, GRAD_WIDE)
        slot = k % 2
        if k >= 2:
            for copy in stores[k - 2]:
                copy.wait()
        keep_ref[slot] = jnp.where(core == 0, part[:, 0], part[:, 1])
        send_ref[slot] = jnp.where(core == 0, part[:, 1], part[:, 0]).astype(jnp.bfloat16)
        stores.append(
            (
                pltpu.make_async_copy(
                    keep_ref.at[slot], keep_far.at[:, :, cols], out_sems.at[0, slot]
                ),
                pltpu.make_async_copy(
                    send_ref.at[slot], send_far.at[:, :, cols], out_sems.at[1, slot]
                ),
            )
        )
        for copy in stores[k]:
            copy.start()
    low = low.astype(jnp.float32)
    feat = acc_ref[...]
    inner = jnp.sum(low * feat, axis=1, keepdims=True)
    feat = (feat - low * inner).astype(jnp.bfloat16)
    count = feat_ref.shape[0]
    share = rows // count
    spot = diagonal(share, LANES)
    for p in range(count):
        mine = slice(p * share, (p + 1) * share)
        feat_ref[p, pl.ds(0, share), :] = feat[mine, :LANES]
        feat_ref[p, pl.ds(share, share), :] = feat[mine, LANES:]
        along = jnp.sum(jnp.where(spot, inner[mine], 0.0), axis=0, keepdims=True)
        feat_ref[p, pl.ds(2 * share, BLOCK), :] = jnp.broadcast_to(along, (BLOCK, LANES)).astype(
            jnp.bfloat16
        )
    last = pltpu.make_async_copy(feat_ref, feat_far, out_sems.at[2, 0])
    last.start()
    for pair in stores[-2:]:
        for copy in pair:
            copy.wait()
    last.wait()


def exchange(copies, axis):
    return lax.all_to_all(copies, axis, 0, 0, tiled=True)


def spread_sum(parts, axis, dim, me, target, dtype=jnp.float32):
    total = lax.dynamic_index_in_dim(parts, me, dim, keepdims=False)
    for hop in HOPS:
        part = lax.dynamic_index_in_dim(parts, (me + hop) % 4, dim, keepdims=False).astype(dtype)
        got = lax.ppermute(part, axis, [(i, target(i, hop)) for i in range(16)])
        total = total + got.astype(jnp.float32)
    return total


def on_device(
    teacher_hidden,
    student_hidden,
    teacher_bottleneck,
    student_bottleneck,
    teacher_prototypes,
    student_prototypes,
):
    f32, bf16 = jnp.float32, jnp.bfloat16
    shape = jax.ShapeDtypeStruct
    rows = teacher_hidden.shape[0]
    columns = teacher_prototypes.shape[1]
    width = teacher_prototypes.shape[0]
    row_tiles, col_tiles = rows // LANES, columns // LANES
    n_dp, n_proto = lax.axis_size("dp"), lax.axis_size("proto")

    def blocks_of(part, count):
        return part.astype(bf16).reshape(count, part.shape[0] // count, part.shape[1])

    teach_part = jnp.dot(teacher_hidden, teacher_bottleneck, preferred_element_type=f32)
    got = exchange(blocks_of(teach_part, n_proto), "proto")

    me, where = lax.axis_index("proto"), lax.axis_index("dp")
    core, high, y_at = jnp.reshape(where % 2, (1,)), (where // 2) % 2, where // 4
    share = rows // n_proto
    teach_norm = col_scales(teacher_prototypes)
    stud_norm = col_scales(student_prototypes)
    own, *sends = on_core(
        parts_kernel,
        [shape((4, share, width), f32)] * 4,
        (jnp.reshape(me % 4, (1,)), student_hidden, student_bottleneck),
        scratch=[pltpu.VMEM((n_proto, share, width), f32)],
        smem=(0,),
    )
    line = [own]
    for hop, part in zip(HOPS, sends):
        line.append(
            lax.ppermute(part, "proto", [(i, i // 4 * 4 + (i + hop) % 4) for i in range(16)])
        )

    (copies,) = on_core(share_kernel, [shape(got.shape, bf16)], (got,))
    copies, teach_norm, stud_norm, line[0] = lax.optimization_barrier(
        (copies, teach_norm, stud_norm, own)
    )
    teach_low = exchange(copies, "proto").reshape(rows, width)
    teach_wlow = (teacher_prototypes.astype(f32) * teach_norm).astype(bf16)
    stud_wlow = (student_prototypes.astype(f32) * stud_norm).astype(bf16)
    stud_share, *sends = on_core(
        line_kernel,
        [shape((share, width), f32)] * 4,
        [jnp.reshape(me // 4, (1,))] + line + [copies],
        scratch=[pltpu.VMEM((4, share, width), f32)],
        smem=(0,),
        far=(5,),
    )
    teach_wlow, stud_wlow, *sends = lax.optimization_barrier((teach_wlow, stud_wlow, *sends))
    for hop, part in zip(HOPS, sends):
        stud_share = stud_share + lax.ppermute(
            part, "proto", [(i, (i + 4 * hop) % 16) for i in range(16)]
        )

    teach_low, teach_wlow, stud_norm, stud_wlow, stud_share, core, high, y_at = (
        lax.optimization_barrier(
            (teach_low, teach_wlow, stud_norm, stud_wlow, stud_share, core, high, y_at)
        )
    )

    big = pltpu.VMEM((rows, columns), KEEP)
    row_acc = [pltpu.VMEM((rows, LANES), f32), pltpu.VMEM((8, LANES), f32)]
    col_sums = pltpu.VMEM((col_tiles, LANES), f32)
    expo, copies = on_core(
        teacher_kernel,
        [big, shape((n_dp, col_tiles, LANES), bf16)],
        (teach_low, teach_wlow),
        scratch=[col_sums],
    )
    for step in range(ITERS):
        got_cols = exchange(copies, "dp")
        count, extra = BLOCK, ()
        if step == ITERS - 2:
            count, extra = BLOCK + 2 * share, (stud_share,)
        if step == ITERS - 1:
            got_rows, got_cols = lax.optimization_barrier((got_rows, got_cols))
            stud_expo, totals, stud_low = on_core(
                student_kernel,
                [
                    pltpu.VMEM((rows, columns), bf16),
                    shape((1, BLOCK, LANES), bf16),
                    shape((rows, width), bf16),
                ],
                (got_rows, stud_wlow),
                scratch=row_acc,
            )
            count, extra = 2 * BLOCK, (totals,)
        (copies,) = on_core(
            row_kernel,
            [shape((n_proto, count, LANES), bf16)],
            (expo, got_cols) + extra,
            scratch=[col_sums] + row_acc,
            pinned=(0,),
        )
        got_rows = exchange(copies, "proto")
        if step < ITERS - 1:
            (copies,) = on_core(
                col_kernel,
                [shape((n_dp, col_tiles, LANES), bf16)],
                (expo, got_rows),
                scratch=[pltpu.VMEM((rows, LANES), f32), col_sums],
                pinned=(0,),
            )

    feat_part, keep, send = on_core(
        grad_kernel,
        [
            pltpu.HBM((n_proto, 2 * share + BLOCK, LANES), bf16),
            pltpu.HBM((8, 16, columns), f32),
            pltpu.HBM((8, 16, columns), bf16),
        ],
        (
            core, expo, stud_expo, stud_low, stud_wlow,
            student_prototypes, stud_norm, got_cols, got_rows,
        ),
        scratch=[
            pltpu.VMEM((n_proto, 2 * share + BLOCK, LANES), bf16),
            pltpu.VMEM((2, 8, 16, GRAD_WIDE), f32),
            pltpu.VMEM((2, 8, 16, GRAD_WIDE), bf16),
            pltpu.SemaphoreType.DMA((3, 2)),
            pltpu.VMEM((rows, LANES), f32),
            pltpu.VMEM((rows, LANES), f32),
            pltpu.VMEM((col_tiles, LANES), f32),
            pltpu.VMEM((rows, width), f32),
        ],
        pinned=(1, 2),
        smem=(0,),
        far_outs=(0, 1, 2),
    )

    got = exchange(feat_part, "proto")
    (copies,) = on_core(proj_kernel, [shape((n_proto, share, width), bf16)], (got, stud_share))
    proj_grad = exchange(copies, "proto").reshape(rows, width)
    got = lax.ppermute(send, "dp", [(i, i ^ 1) for i in range(16)])
    pair = (keep + got.astype(f32)).reshape(4, 2, 16, columns)
    quarter = spread_sum(pair, "dp", 0, y_at, lambda i, hop: (i + 4 * hop) % 16, bf16)
    proj_grad, quarter = lax.optimization_barrier((proj_grad, quarter))
    keep = jnp.where(high == 0, quarter[0], quarter[1])
    send = jnp.where(high == 0, quarter[1], quarter[0]).astype(bf16)
    got = lax.ppermute(send, "dp", [(i, i ^ 2) for i in range(16)])
    grad_prototypes = keep + got.astype(f32)
    bottle_part = lax.dot_general(
        proj_grad, student_hidden, (((0,), (0,)), ((), ())), preferred_element_type=f32
    )
    got_bottle = exchange(blocks_of(bottle_part, n_dp), "dp")
    grad_bottleneck = jnp.sum(got_bottle.astype(f32), axis=0).T

    return (grad_prototypes, grad_bottleneck)


def solution(mesh):
    return jax.shard_map(
        on_device,
        mesh=mesh,
        in_specs=(
            P("dp", "proto"),
            P("dp", "proto"),
            P("proto", None),
            P("proto", None),
            P(None, "proto"),
            P(None, "proto"),
        ),
        out_specs=(P("dp", "proto"), P("proto", "dp")),
        check_vma=False,
    )
```

```python
import functools

import jax
import jax.numpy as jnp
from jax import lax
from jax.experimental import pallas as pl
from jax.experimental.pallas import tpu as pltpu
from jax.sharding import PartitionSpec as P

PROTOS = 65536
ITERS = 3

TEACHER_TEMP = 0.07
STUDENT_TEMP = 0.1
EPSILON = 1e-06
LOG2E = 1.4426950408889634

LANES = 128
WIDE = 512
GRAD_WIDE = 1024
LIMIT = 16 * 2**20
KEEP = jnp.float32
HOPS = (2, 1, 3)
BLOCK = 16


def unit_rows(values):
    scale = lax.rsqrt(jnp.sum(values * values, axis=1, keepdims=True) + EPSILON)
    return (values * scale, scale)


def col_scales(weights):
    values = weights.astype(jnp.float32)
    return lax.rsqrt(jnp.sum(values * values, axis=0, keepdims=True) + EPSILON)


def on_core(kernel, outs, args, scratch=(), pinned=(), smem=(), far=(), far_outs=()):
    args = [
        pltpu.with_memory_space_constraint(a, pltpu.VMEM if i in pinned else pltpu.HBM)
        if i in pinned or i in far
        else a
        for i, a in enumerate(args)
    ]

    def place(i, far_ones):
        return pl.BlockSpec(memory_space=pltpu.HBM if i in far_ones else pltpu.VMEM)

    return pl.pallas_call(
        kernel,
        out_shape=tuple(outs),
        in_specs=[
            pl.BlockSpec(memory_space=pltpu.SMEM) if i in smem else place(i, far)
            for i in range(len(args))
        ],
        out_specs=tuple(place(i, far_outs) for i in range(len(outs))),
        scratch_shapes=list(scratch),
        compiler_params=pltpu.CompilerParams(vmem_limit_bytes=LIMIT),
    )(*args)


def column_of(rows, j):
    return jnp.broadcast_to(rows[j : j + 1, :], (LANES, LANES)).T


def put_row_sums(acc_ref, out_ref, sums_ref):
    sums_ref[...] = jnp.zeros_like(sums_ref)
    for j in range(acc_ref.shape[0] // LANES):
        sums_ref[pl.ds(j, 1), :] = jnp.sum(
            acc_ref[pl.ds(j * LANES, LANES), :].T, axis=0, keepdims=True
        )
    sums = sums_ref[...]
    high = sums.astype(jnp.bfloat16).astype(jnp.float32)
    block = jnp.concatenate([high, sums - high], axis=0).astype(jnp.bfloat16)
    for p in range(out_ref.shape[0]):
        out_ref[p, pl.ds(0, BLOCK), :] = block


def get_row_sums(got_ref, first):
    terms = jnp.sum(got_ref[:, pl.ds(first, BLOCK), :].astype(jnp.float32), axis=0)
    return terms[:8] + terms[8:]


def diagonal(rows, columns):
    shape = (rows, columns)
    return lax.broadcasted_iota(jnp.int32, shape, 0) == lax.broadcasted_iota(jnp.int32, shape, 1)


def share_kernel(got_ref, out_ref):
    unit, unused_scale = unit_rows(jnp.sum(got_ref[...].astype(jnp.float32), axis=0))
    unit = unit.astype(out_ref.dtype)
    for p in range(out_ref.shape[0]):
        out_ref[p] = unit


def parts_kernel(at_ref, hidden_ref, weight_ref, *refs):
    part_ref = refs[-1]
    count, share, width = part_ref.shape
    part = jnp.dot(hidden_ref[...], weight_ref[...], preferred_element_type=jnp.float32)
    part_ref[...] = part.reshape(count, share, width)
    for out_ref, hop in zip(refs[:-1], (0,) + HOPS):
        for line in range(4):
            out_ref[line] = part_ref[line * 4 + ((at_ref[0] + hop) & 3)]


def line_kernel(at_ref, own_ref, one_ref, two_ref, three_ref, unused_ref, *refs):
    sum_ref = refs[-1]
    sum_ref[...] = own_ref[...] + one_ref[...] + two_ref[...] + three_ref[...]
    for out_ref, hop in zip(refs[:-1], (0,) + HOPS):
        out_ref[...] = sum_ref[(at_ref[0] + hop) & 3]


def proj_kernel(got_ref, share_ref, out_ref):
    unit, scale = unit_rows(share_ref[...])
    share = unit.shape[0]
    got = jnp.sum(got_ref[...].astype(jnp.float32), axis=0)
    along = jnp.where(diagonal(share, LANES), got[2 * share : 2 * share + 1], 0.0)
    low = unit.astype(jnp.bfloat16).astype(jnp.float32)
    feat = jnp.concatenate([got[:share], got[share : 2 * share]], axis=1)
    feat = feat + low * jnp.sum(along, axis=1, keepdims=True)
    inner = jnp.sum(unit * feat, axis=1, keepdims=True)
    rows = (scale * (feat - unit * inner)).astype(out_ref.dtype)
    for p in range(out_ref.shape[0]):
        out_ref[p] = rows


def teacher_kernel(low_ref, w_ref, expo_ref, out_ref, sums_ref):
    low = low_ref[...]
    for k in range(w_ref.shape[1] // WIDE):
        cols = pl.ds(k * WIDE, WIDE)
        scores = jnp.dot(low, w_ref[:, cols], preferred_element_type=jnp.float32)
        expo = jnp.exp2(scores * (LOG2E / TEACHER_TEMP))
        expo_ref[:, cols] = expo.astype(expo_ref.dtype)
        sums = jnp.sum(expo, axis=0, keepdims=True)
        for t in range(WIDE // LANES):
            sums_ref[pl.ds(k * (WIDE // LANES) + t, 1), :] = sums[:, t * LANES : (t + 1) * LANES]
    sums = sums_ref[...].astype(out_ref.dtype)
    for p in range(out_ref.shape[0]):
        out_ref[p] = sums


def student_kernel(first_ref, second_ref, w_ref, expo_ref, totals_ref, low_ref, acc_ref, sums_ref):
    share = first_ref.shape[1] - BLOCK
    for p in range(first_ref.shape[0]):
        for half, got_ref in enumerate((first_ref, second_ref)):
            low_ref[pl.ds(p * share, share), pl.ds(half * LANES, LANES)] = got_ref[
                p, pl.ds(BLOCK, share), :
            ]
    low = low_ref[...]
    for k in range(w_ref.shape[1] // WIDE):
        cols = pl.ds(k * WIDE, WIDE)
        scores = jnp.dot(low, w_ref[:, cols], preferred_element_type=jnp.float32)
        expo = jnp.exp2(scores * (LOG2E / STUDENT_TEMP))
        expo_ref[:, cols] = expo.astype(expo_ref.dtype)
        part = sum(expo[:, t * LANES : (t + 1) * LANES] for t in range(WIDE // LANES))
        acc_ref[...] = part if k == 0 else acc_ref[...] + part
    put_row_sums(acc_ref, totals_ref, sums_ref)


def row_kernel(half, expo_ref, got_ref, *refs):
    extra_ref = refs[0] if len(refs) == 5 else None
    out_ref, scale_ref, acc_ref, sums_ref = refs[-4:]
    rows, columns = expo_ref.shape
    scale_ref[...] = 1.0 / jnp.sum(got_ref[...].astype(jnp.float32), axis=0)
    block = 64

    def body(i, _):
        at = pl.multiple_of(i * block, block)
        acc = [jnp.zeros((8, LANES), jnp.float32)] * (block // 8)
        for t in range(columns // LANES):
            scale = jnp.broadcast_to(scale_ref[pl.ds(t, 1), :], (8, LANES))
            for r in range(block // 16):
                piece = expo_ref[pl.ds(at + r * 16, 16), pl.ds(t * LANES, LANES)].astype(jnp.float32)
                acc[2 * r] += piece[:8] * scale
                acc[2 * r + 1] += piece[8:] * scale
        for r in range(block // 8):
            acc_ref[pl.ds(at + r * 8, 8), :] = acc[r]
        return 0

    lax.fori_loop(0, rows // block, body, 0)
    put_row_sums(acc_ref, out_ref, sums_ref)
    if extra_ref is not None and len(extra_ref.shape) == 3:
        for p in range(out_ref.shape[0]):
            out_ref[p, pl.ds(BLOCK, BLOCK), :] = extra_ref[0]
    elif extra_ref is not None:
        unit, unused_scale = unit_rows(extra_ref[...])
        unit = unit[:, half * LANES : (half + 1) * LANES].astype(out_ref.dtype)
        for p in range(out_ref.shape[0]):
            out_ref[p, pl.ds(BLOCK, unit.shape[0]), :] = unit


def col_kernel(expo_ref, got_ref, out_ref, scale_ref, sums_ref):
    rows, columns = expo_ref.shape
    scale = 1.0 / get_row_sums(got_ref, 0)
    for j in range(rows // LANES):
        scale_ref[pl.ds(j * LANES, LANES), :] = column_of(scale, j)
    tiles = 8

    for k in range(columns // (tiles * LANES)):

        def body(i, acc):
            acc = list(acc)
            at = pl.multiple_of(i * 64, 64)
            for r in range(4):
                weight = scale_ref[pl.ds(at + r * 16, 16), :]
                for t in range(tiles):
                    lanes = pl.ds((k * tiles + t) * LANES, LANES)
                    piece = expo_ref[pl.ds(at + r * 16, 16), lanes].astype(jnp.float32) * weight
                    acc[t] += piece[:8] + piece[8:]
            return tuple(acc)

        acc = lax.fori_loop(
            0, rows // 64, body, tuple(jnp.zeros((8, LANES), jnp.float32) for _ in range(tiles))
        )
        for t in range(tiles):
            sums_ref[pl.ds(k * tiles + t, 1), :] = jnp.sum(acc[t], axis=0, keepdims=True)
    sums = sums_ref[...].astype(out_ref.dtype)
    for p in range(out_ref.shape[0]):
        out_ref[p] = sums


def grad_kernel(
    core_ref, expo_ref, stud_ref, low_ref, wlow_ref, raw_ref, norm_ref, cols_ref, rows_ref,
    feat_far, keep_far, send_far, feat_ref, keep_ref, send_ref, out_sems,
    assign_ref, prob_ref, colscale_ref, acc_ref,
):
    rows, columns = expo_ref.shape
    factor = PROTOS / 32.0 / STUDENT_TEMP
    by_row = 1.0 / get_row_sums(rows_ref, 0)
    by_total = 1.0 / get_row_sums(rows_ref, BLOCK)
    colscale_ref[...] = 1.0 / jnp.sum(cols_ref[...].astype(jnp.float32), axis=0)
    for j in range(rows // LANES):
        at = pl.ds(j * LANES, LANES)
        assign_ref[at, :] = column_of(by_row, j) * factor
        prob_ref[at, :] = column_of(by_total, j) * factor
    core = core_ref[0]
    low = low_ref[...]
    stores = []
    for k in range(columns // GRAD_WIDE):
        cols = pl.ds(k * GRAD_WIDE, GRAD_WIDE)
        pieces = []
        for t in range(GRAD_WIDE // LANES):
            at = pl.ds(k * GRAD_WIDE + t * LANES, LANES)
            scale = colscale_ref[pl.ds(k * (GRAD_WIDE // LANES) + t, 1), :]
            pieces.append(
                (
                    stud_ref[:, at].astype(jnp.float32) * prob_ref[...]
                    - assign_ref[...] * (expo_ref[:, at].astype(jnp.float32) * scale)
                ).astype(jnp.bfloat16)
            )
        grad = jnp.concatenate(pieces, axis=1)
        feat = lax.dot_general(
            grad, wlow_ref[:, cols], (((1,), (1,)), ((), ())), preferred_element_type=jnp.float32
        )
        acc_ref[...] = feat if k == 0 else acc_ref[...] + feat
        proto = lax.dot_general(
            low, grad, (((0,), (0,)), ((), ())), preferred_element_type=jnp.float32
        )
        norm = norm_ref[:, cols]
        unit = raw_ref[:, cols].astype(jnp.float32) * norm
        dots = jnp.sum(unit * proto, axis=0, keepdims=True)
        part = norm * (proto - unit * dots)
        part = part.reshape(8, 2, 16, GRAD_WIDE)
        slot = k % 2
        if k >= 2:
            for copy in stores[k - 2]:
                copy.wait()
        keep_ref[slot] = jnp.where(core == 0, part[:, 0], part[:, 1])
        send_ref[slot] = jnp.where(core == 0, part[:, 1], part[:, 0]).astype(jnp.bfloat16)
        stores.append(
            (
                pltpu.make_async_copy(
                    keep_ref.at[slot], keep_far.at[:, :, cols], out_sems.at[0, slot]
                ),
                pltpu.make_async_copy(
                    send_ref.at[slot], send_far.at[:, :, cols], out_sems.at[1, slot]
                ),
            )
        )
        for copy in stores[k]:
            copy.start()
    low = low.astype(jnp.float32)
    feat = acc_ref[...]
    inner = jnp.sum(low * feat, axis=1, keepdims=True)
    feat = (feat - low * inner).astype(jnp.bfloat16)
    count = feat_ref.shape[0]
    share = rows // count
    spot = diagonal(share, LANES)
    for p in range(count):
        mine = slice(p * share, (p + 1) * share)
        feat_ref[p, pl.ds(0, share), :] = feat[mine, :LANES]
        feat_ref[p, pl.ds(share, share), :] = feat[mine, LANES:]
        along = jnp.sum(jnp.where(spot, inner[mine], 0.0), axis=0, keepdims=True)
        feat_ref[p, pl.ds(2 * share, BLOCK), :] = jnp.broadcast_to(along, (BLOCK, LANES)).astype(
            jnp.bfloat16
        )
    last = pltpu.make_async_copy(feat_ref, feat_far, out_sems.at[2, 0])
    last.start()
    for pair in stores[-2:]:
        for copy in pair:
            copy.wait()
    last.wait()


def exchange(copies, axis):
    return lax.all_to_all(copies, axis, 0, 0, tiled=True)


def spread_sum(parts, axis, dim, me, target, dtype=jnp.float32):
    total = lax.dynamic_index_in_dim(parts, me, dim, keepdims=False)
    for hop in HOPS:
        part = lax.dynamic_index_in_dim(parts, (me + hop) % 4, dim, keepdims=False).astype(dtype)
        got = lax.ppermute(part, axis, [(i, target(i, hop)) for i in range(16)])
        total = total + got.astype(jnp.float32)
    return total


def on_device(
    teacher_hidden,
    student_hidden,
    teacher_bottleneck,
    student_bottleneck,
    teacher_prototypes,
    student_prototypes,
):
    f32, bf16 = jnp.float32, jnp.bfloat16
    shape = jax.ShapeDtypeStruct
    rows = teacher_hidden.shape[0]
    columns = teacher_prototypes.shape[1]
    width = teacher_prototypes.shape[0]
    row_tiles, col_tiles = rows // LANES, columns // LANES
    n_dp, n_proto = lax.axis_size("dp"), lax.axis_size("proto")

    def blocks_of(part, count):
        return part.astype(bf16).reshape(count, part.shape[0] // count, part.shape[1])

    teach_part = jnp.dot(teacher_hidden, teacher_bottleneck, preferred_element_type=f32)
    got = exchange(blocks_of(teach_part, n_proto), "proto")

    me, where = lax.axis_index("proto"), lax.axis_index("dp")
    core, high, y_at = jnp.reshape(where % 2, (1,)), (where // 2) % 2, where // 4
    share = rows // n_proto
    teach_norm = col_scales(teacher_prototypes)
    stud_norm = col_scales(student_prototypes)
    own, *sends = on_core(
        parts_kernel,
        [shape((4, share, width), f32)] * 4,
        (jnp.reshape(me % 4, (1,)), student_hidden, student_bottleneck),
        scratch=[pltpu.VMEM((n_proto, share, width), f32)],
        smem=(0,),
    )
    line = [own]
    for hop, part in zip(HOPS, sends):
        line.append(
            lax.ppermute(part, "proto", [(i, i // 4 * 4 + (i + hop) % 4) for i in range(16)])
        )

    (copies,) = on_core(share_kernel, [shape(got.shape, bf16)], (got,))
    copies, teach_norm, stud_norm, line[0] = lax.optimization_barrier(
        (copies, teach_norm, stud_norm, own)
    )
    teach_low = exchange(copies, "proto").reshape(rows, width)
    teach_wlow = (teacher_prototypes.astype(f32) * teach_norm).astype(bf16)
    stud_wlow = (student_prototypes.astype(f32) * stud_norm).astype(bf16)
    stud_share, *sends = on_core(
        line_kernel,
        [shape((share, width), f32)] * 4,
        [jnp.reshape(me // 4, (1,))] + line + [copies],
        scratch=[pltpu.VMEM((4, share, width), f32)],
        smem=(0,),
        far=(5,),
    )
    for hop, part in zip(HOPS, sends):
        stud_share = stud_share + lax.ppermute(
            part, "proto", [(i, (i + 4 * hop) % 16) for i in range(16)]
        )

    teach_low, teach_wlow, stud_norm, stud_wlow, stud_share, core, high, y_at = (
        lax.optimization_barrier(
            (teach_low, teach_wlow, stud_norm, stud_wlow, stud_share, core, high, y_at)
        )
    )

    big = pltpu.VMEM((rows, columns), KEEP)
    row_acc = [pltpu.VMEM((rows, LANES), f32), pltpu.VMEM((8, LANES), f32)]
    col_sums = pltpu.VMEM((col_tiles, LANES), f32)
    expo, copies = on_core(
        teacher_kernel,
        [big, shape((n_dp, col_tiles, LANES), bf16)],
        (teach_low, teach_wlow),
        scratch=[col_sums],
    )
    halves = []
    for step in range(ITERS):
        got_cols = exchange(copies, "dp")
        count, extra = BLOCK, ()
        if step < ITERS - 1:
            count, extra = BLOCK + share, (stud_share,)
        if step == ITERS - 1:
            halves[1], got_cols = lax.optimization_barrier((halves[1], got_cols))
            stud_expo, totals, stud_low = on_core(
                student_kernel,
                [
                    pltpu.VMEM((rows, columns), bf16),
                    shape((1, BLOCK, LANES), bf16),
                    shape((rows, width), bf16),
                ],
                (*halves, stud_wlow),
                scratch=row_acc,
            )
            count, extra = 2 * BLOCK, (totals,)
        (copies,) = on_core(
            functools.partial(row_kernel, step),
            [shape((n_proto, count, LANES), bf16)],
            (expo, got_cols) + extra,
            scratch=[col_sums] + row_acc,
            pinned=(0,),
        )
        got_rows = exchange(copies, "proto")
        halves.append(got_rows)
        if step < ITERS - 1:
            (copies,) = on_core(
                col_kernel,
                [shape((n_dp, col_tiles, LANES), bf16)],
                (expo, got_rows),
                scratch=[pltpu.VMEM((rows, LANES), f32), col_sums],
                pinned=(0,),
            )

    feat_part, keep, send = on_core(
        grad_kernel,
        [
            pltpu.HBM((n_proto, 2 * share + BLOCK, LANES), bf16),
            pltpu.HBM((8, 16, columns), f32),
            pltpu.HBM((8, 16, columns), bf16),
        ],
        (
            core, expo, stud_expo, stud_low, stud_wlow,
            student_prototypes, stud_norm, got_cols, got_rows,
        ),
        scratch=[
            pltpu.VMEM((n_proto, 2 * share + BLOCK, LANES), bf16),
            pltpu.VMEM((2, 8, 16, GRAD_WIDE), f32),
            pltpu.VMEM((2, 8, 16, GRAD_WIDE), bf16),
            pltpu.SemaphoreType.DMA((3, 2)),
            pltpu.VMEM((rows, LANES), f32),
            pltpu.VMEM((rows, LANES), f32),
            pltpu.VMEM((col_tiles, LANES), f32),
            pltpu.VMEM((rows, width), f32),
        ],
        pinned=(1, 2),
        smem=(0,),
        far_outs=(0, 1, 2),
    )

    got = exchange(feat_part, "proto")
    (copies,) = on_core(proj_kernel, [shape((n_proto, share, width), bf16)], (got, stud_share))
    proj_grad = exchange(copies, "proto").reshape(rows, width)
    got = lax.ppermute(send, "dp", [(i, i ^ 1) for i in range(16)])
    pair = (keep + got.astype(f32)).reshape(4, 2, 16, columns)
    quarter = spread_sum(pair, "dp", 0, y_at, lambda i, hop: (i + 4 * hop) % 16, bf16)
    proj_grad, quarter = lax.optimization_barrier((proj_grad, quarter))
    keep = jnp.where(high == 0, quarter[0], quarter[1])
    send = jnp.where(high == 0, quarter[1], quarter[0]).astype(bf16)
    got = lax.ppermute(send, "dp", [(i, i ^ 2) for i in range(16)])
    grad_prototypes = keep + got.astype(f32)
    bottle_part = lax.dot_general(
        proj_grad, student_hidden, (((0,), (0,)), ((), ())), preferred_element_type=f32
    )
    got_bottle = exchange(blocks_of(bottle_part, n_dp), "dp")
    grad_bottleneck = jnp.sum(got_bottle.astype(f32), axis=0).T

    return (grad_prototypes, grad_bottleneck)


def solution(mesh):
    return jax.shard_map(
        on_device,
        mesh=mesh,
        in_specs=(
            P("dp", "proto"),
            P("dp", "proto"),
            P("proto", None),
            P("proto", None),
            P(None, "proto"),
            P(None, "proto"),
        ),
        out_specs=(P("dp", "proto"), P("proto", "dp")),
        check_vma=False,
    )
```

```python
import functools

import jax
import jax.numpy as jnp
from jax import lax
from jax.experimental import pallas as pl
from jax.experimental.pallas import tpu as pltpu
from jax.sharding import PartitionSpec as P

PROTOS = 65536
ITERS = 3

TEACHER_TEMP = 0.07
STUDENT_TEMP = 0.1
EPSILON = 1e-06
LOG2E = 1.4426950408889634

LANES = 128
WIDE = 512
GRAD_WIDE = 1024
LIMIT = 16 * 2**20
KEEP = jnp.float32
HOPS = (2, 1, 3)
BLOCK = 16


def unit_rows(values):
    scale = lax.rsqrt(jnp.sum(values * values, axis=1, keepdims=True) + EPSILON)
    return (values * scale, scale)


def col_scales(weights):
    values = weights.astype(jnp.float32)
    return lax.rsqrt(jnp.sum(values * values, axis=0, keepdims=True) + EPSILON)


def on_core(kernel, outs, args, scratch=(), pinned=(), smem=(), far=(), far_outs=()):
    args = [
        pltpu.with_memory_space_constraint(a, pltpu.VMEM if i in pinned else pltpu.HBM)
        if i in pinned or i in far
        else a
        for i, a in enumerate(args)
    ]

    def place(i, far_ones):
        return pl.BlockSpec(memory_space=pltpu.HBM if i in far_ones else pltpu.VMEM)

    return pl.pallas_call(
        kernel,
        out_shape=tuple(outs),
        in_specs=[
            pl.BlockSpec(memory_space=pltpu.SMEM) if i in smem else place(i, far)
            for i in range(len(args))
        ],
        out_specs=tuple(place(i, far_outs) for i in range(len(outs))),
        scratch_shapes=list(scratch),
        compiler_params=pltpu.CompilerParams(vmem_limit_bytes=LIMIT),
    )(*args)


def column_of(rows, j):
    return jnp.broadcast_to(rows[j : j + 1, :], (LANES, LANES)).T


def put_row_sums(acc_ref, out_ref, sums_ref):
    sums_ref[...] = jnp.zeros_like(sums_ref)
    for j in range(acc_ref.shape[0] // LANES):
        sums_ref[pl.ds(j, 1), :] = jnp.sum(
            acc_ref[pl.ds(j * LANES, LANES), :].T, axis=0, keepdims=True
        )
    sums = sums_ref[...]
    high = sums.astype(jnp.bfloat16).astype(jnp.float32)
    block = jnp.concatenate([high, sums - high], axis=0).astype(jnp.bfloat16)
    for p in range(out_ref.shape[0]):
        out_ref[p, pl.ds(0, BLOCK), :] = block


def get_row_sums(got_ref, first):
    terms = jnp.sum(got_ref[:, pl.ds(first, BLOCK), :].astype(jnp.float32), axis=0)
    return terms[:8] + terms[8:]


def diagonal(rows, columns):
    shape = (rows, columns)
    return lax.broadcasted_iota(jnp.int32, shape, 0) == lax.broadcasted_iota(jnp.int32, shape, 1)


def fetch(far_refs, near_refs, sems):
    copies = [
        pltpu.make_async_copy(far, near, sems.at[i])
        for i, (far, near) in enumerate(zip(far_refs, near_refs))
    ]
    for copy in copies:
        copy.start()
    for copy in copies:
        copy.wait()


def project_kernel(hidden_far, weight_far, out_ref, hidden_ref, weight_ref, sems):
    fetch((hidden_far, weight_far), (hidden_ref, weight_ref), sems)
    part = jnp.dot(hidden_ref[...], weight_ref[...], preferred_element_type=jnp.float32)
    out_ref[...] = part.astype(out_ref.dtype).reshape(out_ref.shape)


def share_kernel(got_ref, out_ref):
    unit, unused_scale = unit_rows(jnp.sum(got_ref[...].astype(jnp.float32), axis=0))
    unit = unit.astype(out_ref.dtype)
    for p in range(out_ref.shape[0]):
        out_ref[p] = unit


def parts_kernel(at_ref, hidden_far, weight_far, *refs):
    outs, (part_ref, hidden_ref, weight_ref, sems) = refs[:4], refs[4:]
    count, share, width = part_ref.shape
    fetch((hidden_far, weight_far), (hidden_ref, weight_ref), sems)
    part = jnp.dot(hidden_ref[...], weight_ref[...], preferred_element_type=jnp.float32)
    part_ref[...] = part.reshape(count, share, width)
    for out_ref, hop in zip(outs, (0,) + HOPS):
        for line in range(4):
            out_ref[line] = part_ref[line * 4 + ((at_ref[0] + hop) & 3)]


def line_kernel(at_ref, own_ref, one_ref, two_ref, three_ref, unused_ref, *refs):
    sum_ref = refs[-1]
    sum_ref[...] = own_ref[...] + one_ref[...] + two_ref[...] + three_ref[...]
    for out_ref, hop in zip(refs[:-1], (0,) + HOPS):
        out_ref[...] = sum_ref[(at_ref[0] + hop) & 3]


def proj_kernel(got_ref, share_ref, out_ref):
    unit, scale = unit_rows(share_ref[...])
    share = unit.shape[0]
    got = jnp.sum(got_ref[...].astype(jnp.float32), axis=0)
    along = jnp.where(diagonal(share, LANES), got[2 * share : 2 * share + 1], 0.0)
    low = unit.astype(jnp.bfloat16).astype(jnp.float32)
    feat = jnp.concatenate([got[:share], got[share : 2 * share]], axis=1)
    feat = feat + low * jnp.sum(along, axis=1, keepdims=True)
    inner = jnp.sum(unit * feat, axis=1, keepdims=True)
    rows = (scale * (feat - unit * inner)).astype(out_ref.dtype)
    for p in range(out_ref.shape[0]):
        out_ref[p] = rows


def teacher_kernel(low_ref, w_ref, expo_ref, out_ref, sums_ref):
    low = low_ref[...]
    for k in range(w_ref.shape[1] // WIDE):
        cols = pl.ds(k * WIDE, WIDE)
        scores = jnp.dot(low, w_ref[:, cols], preferred_element_type=jnp.float32)
        expo = jnp.exp2(scores * (LOG2E / TEACHER_TEMP))
        expo_ref[:, cols] = expo.astype(expo_ref.dtype)
        sums = jnp.sum(expo, axis=0, keepdims=True)
        for t in range(WIDE // LANES):
            sums_ref[pl.ds(k * (WIDE // LANES) + t, 1), :] = sums[:, t * LANES : (t + 1) * LANES]
    sums = sums_ref[...].astype(out_ref.dtype)
    for p in range(out_ref.shape[0]):
        out_ref[p] = sums


def student_kernel(first_ref, second_ref, w_ref, expo_ref, totals_ref, low_ref, acc_ref, sums_ref):
    share = first_ref.shape[1] - BLOCK
    for p in range(first_ref.shape[0]):
        for half, got_ref in enumerate((first_ref, second_ref)):
            low_ref[pl.ds(p * share, share), pl.ds(half * LANES, LANES)] = got_ref[
                p, pl.ds(BLOCK, share), :
            ]
    low = low_ref[...]
    for k in range(w_ref.shape[1] // WIDE):
        cols = pl.ds(k * WIDE, WIDE)
        scores = jnp.dot(low, w_ref[:, cols], preferred_element_type=jnp.float32)
        expo = jnp.exp2(scores * (LOG2E / STUDENT_TEMP))
        expo_ref[:, cols] = expo.astype(expo_ref.dtype)
        part = sum(expo[:, t * LANES : (t + 1) * LANES] for t in range(WIDE // LANES))
        acc_ref[...] = part if k == 0 else acc_ref[...] + part
    put_row_sums(acc_ref, totals_ref, sums_ref)


def row_kernel(half, expo_ref, got_ref, *refs):
    extra_ref = refs[0] if len(refs) == 5 else None
    out_ref, scale_ref, acc_ref, sums_ref = refs[-4:]
    rows, columns = expo_ref.shape
    scale_ref[...] = 1.0 / jnp.sum(got_ref[...].astype(jnp.float32), axis=0)
    block = 64

    def body(i, _):
        at = pl.multiple_of(i * block, block)
        acc = [jnp.zeros((8, LANES), jnp.float32)] * (block // 8)
        for t in range(columns // LANES):
            scale = jnp.broadcast_to(scale_ref[pl.ds(t, 1), :], (8, LANES))
            for r in range(block // 16):
                piece = expo_ref[pl.ds(at + r * 16, 16), pl.ds(t * LANES, LANES)].astype(jnp.float32)
                acc[2 * r] += piece[:8] * scale
                acc[2 * r + 1] += piece[8:] * scale
        for r in range(block // 8):
            acc_ref[pl.ds(at + r * 8, 8), :] = acc[r]
        return 0

    lax.fori_loop(0, rows // block, body, 0)
    put_row_sums(acc_ref, out_ref, sums_ref)
    if extra_ref is not None and len(extra_ref.shape) == 3:
        for p in range(out_ref.shape[0]):
            out_ref[p, pl.ds(BLOCK, BLOCK), :] = extra_ref[0]
    elif extra_ref is not None:
        unit, unused_scale = unit_rows(extra_ref[...])
        unit = unit[:, half * LANES : (half + 1) * LANES].astype(out_ref.dtype)
        for p in range(out_ref.shape[0]):
            out_ref[p, pl.ds(BLOCK, unit.shape[0]), :] = unit


def col_kernel(expo_ref, got_ref, out_ref, scale_ref, sums_ref):
    rows, columns = expo_ref.shape
    scale = 1.0 / get_row_sums(got_ref, 0)
    for j in range(rows // LANES):
        scale_ref[pl.ds(j * LANES, LANES), :] = column_of(scale, j)
    tiles = 8

    for k in range(columns // (tiles * LANES)):

        def body(i, acc):
            acc = list(acc)
            at = pl.multiple_of(i * 64, 64)
            for r in range(4):
                weight = scale_ref[pl.ds(at + r * 16, 16), :]
                for t in range(tiles):
                    lanes = pl.ds((k * tiles + t) * LANES, LANES)
                    piece = expo_ref[pl.ds(at + r * 16, 16), lanes].astype(jnp.float32) * weight
                    acc[t] += piece[:8] + piece[8:]
            return tuple(acc)

        acc = lax.fori_loop(
            0, rows // 64, body, tuple(jnp.zeros((8, LANES), jnp.float32) for _ in range(tiles))
        )
        for t in range(tiles):
            sums_ref[pl.ds(k * tiles + t, 1), :] = jnp.sum(acc[t], axis=0, keepdims=True)
    sums = sums_ref[...].astype(out_ref.dtype)
    for p in range(out_ref.shape[0]):
        out_ref[p] = sums


def grad_kernel(
    core_ref, expo_ref, stud_ref, low_ref, wlow_ref, raw_ref, norm_ref, cols_ref, rows_ref,
    feat_far, keep_far, send_far, feat_ref, keep_ref, send_ref, out_sems,
    assign_ref, prob_ref, colscale_ref, acc_ref,
):
    rows, columns = expo_ref.shape
    factor = PROTOS / 32.0 / STUDENT_TEMP
    by_row = 1.0 / get_row_sums(rows_ref, 0)
    by_total = 1.0 / get_row_sums(rows_ref, BLOCK)
    colscale_ref[...] = 1.0 / jnp.sum(cols_ref[...].astype(jnp.float32), axis=0)
    for j in range(rows // LANES):
        at = pl.ds(j * LANES, LANES)
        assign_ref[at, :] = column_of(by_row, j) * factor
        prob_ref[at, :] = column_of(by_total, j) * factor
    core = core_ref[0]
    low = low_ref[...]
    stores = []
    for k in range(columns // GRAD_WIDE):
        cols = pl.ds(k * GRAD_WIDE, GRAD_WIDE)
        pieces = []
        for t in range(GRAD_WIDE // LANES):
            at = pl.ds(k * GRAD_WIDE + t * LANES, LANES)
            scale = colscale_ref[pl.ds(k * (GRAD_WIDE // LANES) + t, 1), :]
            pieces.append(
                (
                    stud_ref[:, at].astype(jnp.float32) * prob_ref[...]
                    - assign_ref[...] * (expo_ref[:, at].astype(jnp.float32) * scale)
                ).astype(jnp.bfloat16)
            )
        grad = jnp.concatenate(pieces, axis=1)
        feat = lax.dot_general(
            grad, wlow_ref[:, cols], (((1,), (1,)), ((), ())), preferred_element_type=jnp.float32
        )
        acc_ref[...] = feat if k == 0 else acc_ref[...] + feat
        proto = lax.dot_general(
            low, grad, (((0,), (0,)), ((), ())), preferred_element_type=jnp.float32
        )
        norm = norm_ref[:, cols]
        unit = raw_ref[:, cols].astype(jnp.float32) * norm
        dots = jnp.sum(unit * proto, axis=0, keepdims=True)
        part = norm * (proto - unit * dots)
        part = part.reshape(8, 2, 16, GRAD_WIDE)
        slot = k % 2
        if k >= 2:
            for copy in stores[k - 2]:
                copy.wait()
        keep_ref[slot] = jnp.where(core == 0, part[:, 0], part[:, 1])
        send_ref[slot] = jnp.where(core == 0, part[:, 1], part[:, 0]).astype(jnp.bfloat16)
        stores.append(
            (
                pltpu.make_async_copy(
                    keep_ref.at[slot], keep_far.at[:, :, cols], out_sems.at[0, slot]
                ),
                pltpu.make_async_copy(
                    send_ref.at[slot], send_far.at[:, :, cols], out_sems.at[1, slot]
                ),
            )
        )
        for copy in stores[k]:
            copy.start()
    low = low.astype(jnp.float32)
    feat = acc_ref[...]
    inner = jnp.sum(low * feat, axis=1, keepdims=True)
    feat = (feat - low * inner).astype(jnp.bfloat16)
    count = feat_ref.shape[0]
    share = rows // count
    spot = diagonal(share, LANES)
    for p in range(count):
        mine = slice(p * share, (p + 1) * share)
        feat_ref[p, pl.ds(0, share), :] = feat[mine, :LANES]
        feat_ref[p, pl.ds(share, share), :] = feat[mine, LANES:]
        along = jnp.sum(jnp.where(spot, inner[mine], 0.0), axis=0, keepdims=True)
        feat_ref[p, pl.ds(2 * share, BLOCK), :] = jnp.broadcast_to(along, (BLOCK, LANES)).astype(
            jnp.bfloat16
        )
    last = pltpu.make_async_copy(feat_ref, feat_far, out_sems.at[2, 0])
    last.start()
    for pair in stores[-2:]:
        for copy in pair:
            copy.wait()
    last.wait()


def exchange(copies, axis):
    return lax.all_to_all(copies, axis, 0, 0, tiled=True)


def spread_sum(parts, axis, dim, me, target, dtype=jnp.float32):
    total = lax.dynamic_index_in_dim(parts, me, dim, keepdims=False)
    for hop in HOPS:
        part = lax.dynamic_index_in_dim(parts, (me + hop) % 4, dim, keepdims=False).astype(dtype)
        got = lax.ppermute(part, axis, [(i, target(i, hop)) for i in range(16)])
        total = total + got.astype(jnp.float32)
    return total


def on_device(
    teacher_hidden,
    student_hidden,
    teacher_bottleneck,
    student_bottleneck,
    teacher_prototypes,
    student_prototypes,
):
    f32, bf16 = jnp.float32, jnp.bfloat16
    shape = jax.ShapeDtypeStruct
    rows = teacher_hidden.shape[0]
    columns = teacher_prototypes.shape[1]
    width = teacher_prototypes.shape[0]
    row_tiles, col_tiles = rows // LANES, columns // LANES
    n_dp, n_proto = lax.axis_size("dp"), lax.axis_size("proto")

    def blocks_of(part, count):
        return part.astype(bf16).reshape(count, part.shape[0] // count, part.shape[1])

    share = rows // n_proto
    operands = [
        pltpu.VMEM(teacher_hidden.shape, bf16),
        pltpu.VMEM(teacher_bottleneck.shape, bf16),
        pltpu.SemaphoreType.DMA((2,)),
    ]
    (blocks,) = on_core(
        project_kernel,
        [shape((n_proto, share, width), bf16)],
        (teacher_hidden, teacher_bottleneck),
        scratch=operands,
        far=(0, 1),
    )
    got = exchange(blocks, "proto")

    me, where = lax.axis_index("proto"), lax.axis_index("dp")
    core, high, y_at = jnp.reshape(where % 2, (1,)), (where // 2) % 2, where // 4
    teach_norm = col_scales(teacher_prototypes)
    stud_norm = col_scales(student_prototypes)
    own, *sends = on_core(
        parts_kernel,
        [shape((4, share, width), f32)] * 4,
        (jnp.reshape(me % 4, (1,)), student_hidden, student_bottleneck),
        scratch=[pltpu.VMEM((n_proto, share, width), f32)] + operands,
        smem=(0,),
        far=(1, 2),
    )
    line = [own]
    for hop, part in zip(HOPS, sends):
        line.append(
            lax.ppermute(part, "proto", [(i, i // 4 * 4 + (i + hop) % 4) for i in range(16)])
        )

    (copies,) = on_core(share_kernel, [shape(got.shape, bf16)], (got,))
    copies, teach_norm, stud_norm, line[0] = lax.optimization_barrier(
        (copies, teach_norm, stud_norm, own)
    )
    teach_low = exchange(copies, "proto").reshape(rows, width)
    teach_wlow = (teacher_prototypes.astype(f32) * teach_norm).astype(bf16)
    stud_wlow = (student_prototypes.astype(f32) * stud_norm).astype(bf16)
    stud_share, *sends = on_core(
        line_kernel,
        [shape((share, width), f32)] * 4,
        [jnp.reshape(me // 4, (1,))] + line + [copies],
        scratch=[pltpu.VMEM((4, share, width), f32)],
        smem=(0,),
        far=(5,),
    )
    for hop, part in zip(HOPS, sends):
        stud_share = stud_share + lax.ppermute(
            part, "proto", [(i, (i + 4 * hop) % 16) for i in range(16)]
        )

    teach_low, teach_wlow, stud_norm, stud_wlow, stud_share, core, high, y_at = (
        lax.optimization_barrier(
            (teach_low, teach_wlow, stud_norm, stud_wlow, stud_share, core, high, y_at)
        )
    )

    big = pltpu.VMEM((rows, columns), KEEP)
    row_acc = [pltpu.VMEM((rows, LANES), f32), pltpu.VMEM((8, LANES), f32)]
    col_sums = pltpu.VMEM((col_tiles, LANES), f32)
    expo, copies = on_core(
        teacher_kernel,
        [big, shape((n_dp, col_tiles, LANES), bf16)],
        (teach_low, teach_wlow),
        scratch=[col_sums],
    )
    halves = []
    for step in range(ITERS):
        got_cols = exchange(copies, "dp")
        count, extra = BLOCK, ()
        if step < ITERS - 1:
            count, extra = BLOCK + share, (stud_share,)
        if step == ITERS - 1:
            halves[1], got_cols = lax.optimization_barrier((halves[1], got_cols))
            stud_expo, totals, stud_low = on_core(
                student_kernel,
                [
                    pltpu.VMEM((rows, columns), bf16),
                    shape((1, BLOCK, LANES), bf16),
                    shape((rows, width), bf16),
                ],
                (*halves, stud_wlow),
                scratch=row_acc,
            )
            count, extra = 2 * BLOCK, (totals,)
        (copies,) = on_core(
            functools.partial(row_kernel, step),
            [shape((n_proto, count, LANES), bf16)],
            (expo, got_cols) + extra,
            scratch=[col_sums] + row_acc,
            pinned=(0,),
        )
        got_rows = exchange(copies, "proto")
        halves.append(got_rows)
        if step < ITERS - 1:
            (copies,) = on_core(
                col_kernel,
                [shape((n_dp, col_tiles, LANES), bf16)],
                (expo, got_rows),
                scratch=[pltpu.VMEM((rows, LANES), f32), col_sums],
                pinned=(0,),
            )

    feat_part, keep, send = on_core(
        grad_kernel,
        [
            pltpu.HBM((n_proto, 2 * share + BLOCK, LANES), bf16),
            pltpu.HBM((8, 16, columns), f32),
            pltpu.HBM((8, 16, columns), bf16),
        ],
        (
            core, expo, stud_expo, stud_low, stud_wlow,
            student_prototypes, stud_norm, got_cols, got_rows,
        ),
        scratch=[
            pltpu.VMEM((n_proto, 2 * share + BLOCK, LANES), bf16),
            pltpu.VMEM((2, 8, 16, GRAD_WIDE), f32),
            pltpu.VMEM((2, 8, 16, GRAD_WIDE), bf16),
            pltpu.SemaphoreType.DMA((3, 2)),
            pltpu.VMEM((rows, LANES), f32),
            pltpu.VMEM((rows, LANES), f32),
            pltpu.VMEM((col_tiles, LANES), f32),
            pltpu.VMEM((rows, width), f32),
        ],
        pinned=(1, 2),
        smem=(0,),
        far_outs=(0, 1, 2),
    )

    got = exchange(feat_part, "proto")
    (copies,) = on_core(proj_kernel, [shape((n_proto, share, width), bf16)], (got, stud_share))
    proj_grad = exchange(copies, "proto").reshape(rows, width)
    got = lax.ppermute(send, "dp", [(i, i ^ 1) for i in range(16)])
    pair = (keep + got.astype(f32)).reshape(4, 2, 16, columns)
    quarter = spread_sum(pair, "dp", 0, y_at, lambda i, hop: (i + 4 * hop) % 16, bf16)
    proj_grad, quarter = lax.optimization_barrier((proj_grad, quarter))
    keep = jnp.where(high == 0, quarter[0], quarter[1])
    send = jnp.where(high == 0, quarter[1], quarter[0]).astype(bf16)
    got = lax.ppermute(send, "dp", [(i, i ^ 2) for i in range(16)])
    grad_prototypes = keep + got.astype(f32)
    bottle_part = lax.dot_general(
        proj_grad, student_hidden, (((0,), (0,)), ((), ())), preferred_element_type=f32
    )
    got_bottle = exchange(blocks_of(bottle_part, n_dp), "dp")
    grad_bottleneck = jnp.sum(got_bottle.astype(f32), axis=0).T

    return (grad_prototypes, grad_bottleneck)


def solution(mesh):
    return jax.shard_map(
        on_device,
        mesh=mesh,
        in_specs=(
            P("dp", "proto"),
            P("dp", "proto"),
            P("proto", None),
            P("proto", None),
            P(None, "proto"),
            P(None, "proto"),
        ),
        out_specs=(P("dp", "proto"), P("proto", "dp")),
        check_vma=False,
    )
```

```python
import functools

import jax
import jax.numpy as jnp
from jax import lax
from jax.experimental import pallas as pl
from jax.experimental.pallas import tpu as pltpu
from jax.sharding import PartitionSpec as P

PROTOS = 65536
ITERS = 3

TEACHER_TEMP = 0.07
STUDENT_TEMP = 0.1
EPSILON = 1e-06
LOG2E = 1.4426950408889634

LANES = 128
WIDE = 512
GRAD_WIDE = 1024
LIMIT = 16 * 2**20
KEEP = jnp.float32
HOPS = (2, 1, 3)
BLOCK = 16


def unit_rows(values):
    scale = lax.rsqrt(jnp.sum(values * values, axis=1, keepdims=True) + EPSILON)
    return (values * scale, scale)


def col_scales(weights):
    values = weights.astype(jnp.float32)
    return lax.rsqrt(jnp.sum(values * values, axis=0, keepdims=True) + EPSILON)


def on_core(kernel, outs, args, scratch=(), pinned=(), smem=(), far=(), far_outs=()):
    args = [
        pltpu.with_memory_space_constraint(a, pltpu.VMEM if i in pinned else pltpu.HBM)
        if i in pinned or i in far
        else a
        for i, a in enumerate(args)
    ]

    def place(i, far_ones):
        return pl.BlockSpec(memory_space=pltpu.HBM if i in far_ones else pltpu.VMEM)

    return pl.pallas_call(
        kernel,
        out_shape=tuple(outs),
        in_specs=[
            pl.BlockSpec(memory_space=pltpu.SMEM) if i in smem else place(i, far)
            for i in range(len(args))
        ],
        out_specs=tuple(place(i, far_outs) for i in range(len(outs))),
        scratch_shapes=list(scratch),
        compiler_params=pltpu.CompilerParams(vmem_limit_bytes=LIMIT),
    )(*args)


def column_of(rows, j):
    return jnp.broadcast_to(rows[j : j + 1, :], (LANES, LANES)).T


def put_row_sums(acc_ref, out_ref, sums_ref):
    sums_ref[...] = jnp.zeros_like(sums_ref)
    for j in range(acc_ref.shape[0] // LANES):
        sums_ref[pl.ds(j, 1), :] = jnp.sum(
            acc_ref[pl.ds(j * LANES, LANES), :].T, axis=0, keepdims=True
        )
    sums = sums_ref[...]
    high = sums.astype(jnp.bfloat16).astype(jnp.float32)
    block = jnp.concatenate([high, sums - high], axis=0).astype(jnp.bfloat16)
    for p in range(out_ref.shape[0]):
        out_ref[p, pl.ds(0, BLOCK), :] = block


def get_row_sums(got_ref, first):
    terms = jnp.sum(got_ref[:, pl.ds(first, BLOCK), :].astype(jnp.float32), axis=0)
    return terms[:8] + terms[8:]


def diagonal(rows, columns):
    shape = (rows, columns)
    return lax.broadcasted_iota(jnp.int32, shape, 0) == lax.broadcasted_iota(jnp.int32, shape, 1)


def fetch(far_refs, near_refs, sems):
    copies = [
        pltpu.make_async_copy(far, near, sems.at[i])
        for i, (far, near) in enumerate(zip(far_refs, near_refs))
    ]
    for copy in copies:
        copy.start()
    for copy in copies:
        copy.wait()


def project_kernel(hidden_far, weight_far, out_ref, hidden_ref, weight_ref, sems):
    fetch((hidden_far, weight_far), (hidden_ref, weight_ref), sems)
    part = jnp.dot(hidden_ref[...], weight_ref[...], preferred_element_type=jnp.float32)
    out_ref[...] = part.astype(out_ref.dtype).reshape(out_ref.shape)


def share_kernel(got_ref, out_ref):
    unit, unused_scale = unit_rows(jnp.sum(got_ref[...].astype(jnp.float32), axis=0))
    unit = unit.astype(out_ref.dtype)
    for p in range(out_ref.shape[0]):
        out_ref[p] = unit


def parts_kernel(at_ref, hidden_far, weight_far, *refs):
    outs, (part_ref, hidden_ref, weight_ref, sems) = refs[:4], refs[4:]
    count, share, width = part_ref.shape
    fetch((hidden_far, weight_far), (hidden_ref, weight_ref), sems)
    part = jnp.dot(hidden_ref[...], weight_ref[...], preferred_element_type=jnp.float32)
    part_ref[...] = part.reshape(count, share, width)
    for out_ref, hop in zip(outs, (0,) + HOPS):
        for line in range(4):
            out_ref[line] = part_ref[line * 4 + ((at_ref[0] + hop) & 3)]


def line_kernel(at_ref, own_ref, one_ref, two_ref, three_ref, unused_ref, *refs):
    sum_ref = refs[-1]
    sum_ref[...] = own_ref[...] + one_ref[...] + two_ref[...] + three_ref[...]
    for out_ref, hop in zip(refs[:-1], (0,) + HOPS):
        out_ref[...] = sum_ref[(at_ref[0] + hop) & 3]


def proj_kernel(got_ref, share_ref, out_ref):
    unit, scale = unit_rows(share_ref[...])
    share = unit.shape[0]
    got = jnp.sum(got_ref[...].astype(jnp.float32), axis=0)
    along = jnp.where(diagonal(share, LANES), got[2 * share : 2 * share + 1], 0.0)
    low = unit.astype(jnp.bfloat16).astype(jnp.float32)
    feat = jnp.concatenate([got[:share], got[share : 2 * share]], axis=1)
    feat = feat + low * jnp.sum(along, axis=1, keepdims=True)
    inner = jnp.sum(unit * feat, axis=1, keepdims=True)
    rows = (scale * (feat - unit * inner)).astype(out_ref.dtype)
    for p in range(out_ref.shape[0]):
        out_ref[p] = rows


def teacher_kernel(low_ref, w_ref, expo_ref, out_ref, sums_ref):
    low = low_ref[...]
    for k in range(w_ref.shape[1] // WIDE):
        cols = pl.ds(k * WIDE, WIDE)
        scores = jnp.dot(low, w_ref[:, cols], preferred_element_type=jnp.float32)
        expo = jnp.exp2(scores * (LOG2E / TEACHER_TEMP))
        expo_ref[:, cols] = expo.astype(expo_ref.dtype)
        sums = jnp.sum(expo, axis=0, keepdims=True)
        for t in range(WIDE // LANES):
            sums_ref[pl.ds(k * (WIDE // LANES) + t, 1), :] = sums[:, t * LANES : (t + 1) * LANES]
    sums = sums_ref[...].astype(out_ref.dtype)
    for p in range(out_ref.shape[0]):
        out_ref[p] = sums


def student_kernel(first_ref, second_ref, w_ref, expo_ref, totals_ref, low_ref, acc_ref, sums_ref):
    share = first_ref.shape[1] - BLOCK
    for p in range(first_ref.shape[0]):
        for half, got_ref in enumerate((first_ref, second_ref)):
            low_ref[pl.ds(p * share, share), pl.ds(half * LANES, LANES)] = got_ref[
                p, pl.ds(BLOCK, share), :
            ]
    low = low_ref[...]
    for k in range(w_ref.shape[1] // WIDE):
        cols = pl.ds(k * WIDE, WIDE)
        scores = jnp.dot(low, w_ref[:, cols], preferred_element_type=jnp.float32)
        expo = jnp.exp2(scores * (LOG2E / STUDENT_TEMP))
        expo_ref[:, cols] = expo.astype(expo_ref.dtype)
        part = sum(expo[:, t * LANES : (t + 1) * LANES] for t in range(WIDE // LANES))
        acc_ref[...] = part if k == 0 else acc_ref[...] + part
    put_row_sums(acc_ref, totals_ref, sums_ref)


def row_kernel(half, expo_ref, got_ref, *refs):
    extra_ref = refs[0] if len(refs) == 5 else None
    out_ref, scale_ref, acc_ref, sums_ref = refs[-4:]
    rows, columns = expo_ref.shape
    scale_ref[...] = 1.0 / jnp.sum(got_ref[...].astype(jnp.float32), axis=0)
    block = 64

    def body(i, _):
        at = pl.multiple_of(i * block, block)
        acc = [jnp.zeros((8, LANES), jnp.float32)] * (block // 8)
        for t in range(columns // LANES):
            scale = jnp.broadcast_to(scale_ref[pl.ds(t, 1), :], (8, LANES))
            for r in range(block // 16):
                piece = expo_ref[pl.ds(at + r * 16, 16), pl.ds(t * LANES, LANES)].astype(jnp.float32)
                acc[2 * r] += piece[:8] * scale
                acc[2 * r + 1] += piece[8:] * scale
        for r in range(block // 8):
            acc_ref[pl.ds(at + r * 8, 8), :] = acc[r]
        return 0

    lax.fori_loop(0, rows // block, body, 0)
    put_row_sums(acc_ref, out_ref, sums_ref)
    if extra_ref is not None and len(extra_ref.shape) == 3:
        for p in range(out_ref.shape[0]):
            out_ref[p, pl.ds(BLOCK, BLOCK), :] = extra_ref[0]
    elif extra_ref is not None:
        unit, unused_scale = unit_rows(extra_ref[...])
        unit = unit[:, half * LANES : (half + 1) * LANES].astype(out_ref.dtype)
        for p in range(out_ref.shape[0]):
            out_ref[p, pl.ds(BLOCK, unit.shape[0]), :] = unit


def col_kernel(expo_ref, got_ref, out_ref, scale_ref, sums_ref):
    rows, columns = expo_ref.shape
    scale = 1.0 / get_row_sums(got_ref, 0)
    for j in range(rows // LANES):
        scale_ref[pl.ds(j * LANES, LANES), :] = column_of(scale, j)
    tiles = 8

    for k in range(columns // (tiles * LANES)):

        def body(i, acc):
            acc = list(acc)
            at = pl.multiple_of(i * 64, 64)
            for r in range(4):
                weight = scale_ref[pl.ds(at + r * 16, 16), :]
                for t in range(tiles):
                    lanes = pl.ds((k * tiles + t) * LANES, LANES)
                    piece = expo_ref[pl.ds(at + r * 16, 16), lanes].astype(jnp.float32) * weight
                    acc[t] += piece[:8] + piece[8:]
            return tuple(acc)

        acc = lax.fori_loop(
            0, rows // 64, body, tuple(jnp.zeros((8, LANES), jnp.float32) for _ in range(tiles))
        )
        for t in range(tiles):
            sums_ref[pl.ds(k * tiles + t, 1), :] = jnp.sum(acc[t], axis=0, keepdims=True)
    sums = sums_ref[...].astype(out_ref.dtype)
    for p in range(out_ref.shape[0]):
        out_ref[p] = sums


def grad_kernel(
    core_ref, expo_ref, stud_ref, low_ref, wlow_ref, raw_ref, norm_ref, cols_ref, rows_ref,
    feat_far, keep_far, send_far, feat_ref, keep_ref, send_ref, out_sems,
    assign_ref, prob_ref, colscale_ref, acc_ref,
):
    rows, columns = expo_ref.shape
    factor = PROTOS / 32.0 / STUDENT_TEMP
    by_row = 1.0 / get_row_sums(rows_ref, 0)
    by_total = 1.0 / get_row_sums(rows_ref, BLOCK)
    colscale_ref[...] = 1.0 / jnp.sum(cols_ref[...].astype(jnp.float32), axis=0)
    for j in range(rows // LANES):
        at = pl.ds(j * LANES, LANES)
        assign_ref[at, :] = column_of(by_row, j) * factor
        prob_ref[at, :] = column_of(by_total, j) * factor
    core = core_ref[0]
    low = low_ref[...]
    stores = []
    for k in range(columns // GRAD_WIDE):
        cols = pl.ds(k * GRAD_WIDE, GRAD_WIDE)
        pieces = []
        for t in range(GRAD_WIDE // LANES):
            at = pl.ds(k * GRAD_WIDE + t * LANES, LANES)
            scale = colscale_ref[pl.ds(k * (GRAD_WIDE // LANES) + t, 1), :]
            pieces.append(
                (
                    stud_ref[:, at].astype(jnp.float32) * prob_ref[...]
                    - assign_ref[...] * (expo_ref[:, at].astype(jnp.float32) * scale)
                ).astype(jnp.bfloat16)
            )
        grad = jnp.concatenate(pieces, axis=1)
        feat = lax.dot_general(
            grad, wlow_ref[:, cols], (((1,), (1,)), ((), ())), preferred_element_type=jnp.float32
        )
        acc_ref[...] = feat if k == 0 else acc_ref[...] + feat
        proto = lax.dot_general(
            low, grad, (((0,), (0,)), ((), ())), preferred_element_type=jnp.float32
        )
        norm = norm_ref[:, cols]
        unit = raw_ref[:, cols].astype(jnp.float32) * norm
        dots = jnp.sum(unit * proto, axis=0, keepdims=True)
        part = norm * (proto - unit * dots)
        part = part.reshape(8, 2, 16, GRAD_WIDE)
        slot = k % 2
        if k >= 2:
            for copy in stores[k - 2]:
                copy.wait()
        keep_ref[slot] = jnp.where(core == 0, part[:, 0], part[:, 1]).astype(jnp.bfloat16)
        send_ref[slot] = jnp.where(core == 0, part[:, 1], part[:, 0]).astype(jnp.bfloat16)
        stores.append(
            (
                pltpu.make_async_copy(
                    keep_ref.at[slot], keep_far.at[:, :, cols], out_sems.at[0, slot]
                ),
                pltpu.make_async_copy(
                    send_ref.at[slot], send_far.at[:, :, cols], out_sems.at[1, slot]
                ),
            )
        )
        for copy in stores[k]:
            copy.start()
    low = low.astype(jnp.float32)
    feat = acc_ref[...]
    inner = jnp.sum(low * feat, axis=1, keepdims=True)
    feat = (feat - low * inner).astype(jnp.bfloat16)
    count = feat_ref.shape[0]
    share = rows // count
    spot = diagonal(share, LANES)
    for p in range(count):
        mine = slice(p * share, (p + 1) * share)
        feat_ref[p, pl.ds(0, share), :] = feat[mine, :LANES]
        feat_ref[p, pl.ds(share, share), :] = feat[mine, LANES:]
        along = jnp.sum(jnp.where(spot, inner[mine], 0.0), axis=0, keepdims=True)
        feat_ref[p, pl.ds(2 * share, BLOCK), :] = jnp.broadcast_to(along, (BLOCK, LANES)).astype(
            jnp.bfloat16
        )
    last = pltpu.make_async_copy(feat_ref, feat_far, out_sems.at[2, 0])
    last.start()
    for pair in stores[-2:]:
        for copy in pair:
            copy.wait()
    last.wait()


def exchange(copies, axis):
    return lax.all_to_all(copies, axis, 0, 0, tiled=True)


def spread_sum(parts, axis, dim, me, target, dtype=jnp.float32):
    total = lax.dynamic_index_in_dim(parts, me, dim, keepdims=False)
    for hop in HOPS:
        part = lax.dynamic_index_in_dim(parts, (me + hop) % 4, dim, keepdims=False).astype(dtype)
        got = lax.ppermute(part, axis, [(i, target(i, hop)) for i in range(16)])
        total = total + got.astype(jnp.float32)
    return total


def on_device(
    teacher_hidden,
    student_hidden,
    teacher_bottleneck,
    student_bottleneck,
    teacher_prototypes,
    student_prototypes,
):
    f32, bf16 = jnp.float32, jnp.bfloat16
    shape = jax.ShapeDtypeStruct
    rows = teacher_hidden.shape[0]
    columns = teacher_prototypes.shape[1]
    width = teacher_prototypes.shape[0]
    row_tiles, col_tiles = rows // LANES, columns // LANES
    n_dp, n_proto = lax.axis_size("dp"), lax.axis_size("proto")

    def blocks_of(part, count):
        return part.astype(bf16).reshape(count, part.shape[0] // count, part.shape[1])

    share = rows // n_proto
    operands = [
        pltpu.VMEM(teacher_hidden.shape, bf16),
        pltpu.VMEM(teacher_bottleneck.shape, bf16),
        pltpu.SemaphoreType.DMA((2,)),
    ]
    (blocks,) = on_core(
        project_kernel,
        [shape((n_proto, share, width), bf16)],
        (teacher_hidden, teacher_bottleneck),
        scratch=operands,
        far=(0, 1),
    )
    got = exchange(blocks, "proto")

    me, where = lax.axis_index("proto"), lax.axis_index("dp")
    core, high, y_at = jnp.reshape(where % 2, (1,)), (where // 2) % 2, where // 4
    teach_norm = col_scales(teacher_prototypes)
    stud_norm = col_scales(student_prototypes)
    own, *sends = on_core(
        parts_kernel,
        [shape((4, share, width), f32)] * 4,
        (jnp.reshape(me % 4, (1,)), student_hidden, student_bottleneck),
        scratch=[pltpu.VMEM((n_proto, share, width), f32)] + operands,
        smem=(0,),
        far=(1, 2),
    )
    line = [own]
    for hop, part in zip(HOPS, sends):
        line.append(
            lax.ppermute(part, "proto", [(i, i // 4 * 4 + (i + hop) % 4) for i in range(16)])
        )

    (copies,) = on_core(share_kernel, [shape(got.shape, bf16)], (got,))
    copies, teach_norm, stud_norm, line[0] = lax.optimization_barrier(
        (copies, teach_norm, stud_norm, own)
    )
    teach_low = exchange(copies, "proto").reshape(rows, width)
    teach_wlow = (teacher_prototypes.astype(f32) * teach_norm).astype(bf16)
    stud_wlow = (student_prototypes.astype(f32) * stud_norm).astype(bf16)
    stud_share, *sends = on_core(
        line_kernel,
        [shape((share, width), f32)] * 4,
        [jnp.reshape(me // 4, (1,))] + line + [copies],
        scratch=[pltpu.VMEM((4, share, width), f32)],
        smem=(0,),
        far=(5,),
    )
    for hop, part in zip(HOPS, sends):
        stud_share = stud_share + lax.ppermute(
            part, "proto", [(i, (i + 4 * hop) % 16) for i in range(16)]
        )

    teach_low, teach_wlow, stud_norm, stud_wlow, stud_share, core, high, y_at = (
        lax.optimization_barrier(
            (teach_low, teach_wlow, stud_norm, stud_wlow, stud_share, core, high, y_at)
        )
    )

    big = pltpu.VMEM((rows, columns), KEEP)
    row_acc = [pltpu.VMEM((rows, LANES), f32), pltpu.VMEM((8, LANES), f32)]
    col_sums = pltpu.VMEM((col_tiles, LANES), f32)
    expo, copies = on_core(
        teacher_kernel,
        [big, shape((n_dp, col_tiles, LANES), bf16)],
        (teach_low, teach_wlow),
        scratch=[col_sums],
    )
    halves = []
    for step in range(ITERS):
        got_cols = exchange(copies, "dp")
        count, extra = BLOCK, ()
        if step < ITERS - 1:
            count, extra = BLOCK + share, (stud_share,)
        if step == ITERS - 1:
            halves[1], got_cols = lax.optimization_barrier((halves[1], got_cols))
            stud_expo, totals, stud_low = on_core(
                student_kernel,
                [
                    pltpu.VMEM((rows, columns), bf16),
                    shape((1, BLOCK, LANES), bf16),
                    shape((rows, width), bf16),
                ],
                (*halves, stud_wlow),
                scratch=row_acc,
            )
            count, extra = 2 * BLOCK, (totals,)
        (copies,) = on_core(
            functools.partial(row_kernel, step),
            [shape((n_proto, count, LANES), bf16)],
            (expo, got_cols) + extra,
            scratch=[col_sums] + row_acc,
            pinned=(0,),
        )
        got_rows = exchange(copies, "proto")
        halves.append(got_rows)
        if step < ITERS - 1:
            (copies,) = on_core(
                col_kernel,
                [shape((n_dp, col_tiles, LANES), bf16)],
                (expo, got_rows),
                scratch=[pltpu.VMEM((rows, LANES), f32), col_sums],
                pinned=(0,),
            )

    feat_part, keep, send = on_core(
        grad_kernel,
        [
            pltpu.HBM((n_proto, 2 * share + BLOCK, LANES), bf16),
            pltpu.HBM((8, 16, columns), bf16),
            pltpu.HBM((8, 16, columns), bf16),
        ],
        (
            core, expo, stud_expo, stud_low, stud_wlow,
            student_prototypes, stud_norm, got_cols, got_rows,
        ),
        scratch=[
            pltpu.VMEM((n_proto, 2 * share + BLOCK, LANES), bf16),
            pltpu.VMEM((2, 8, 16, GRAD_WIDE), bf16),
            pltpu.VMEM((2, 8, 16, GRAD_WIDE), bf16),
            pltpu.SemaphoreType.DMA((3, 2)),
            pltpu.VMEM((rows, LANES), f32),
            pltpu.VMEM((rows, LANES), f32),
            pltpu.VMEM((col_tiles, LANES), f32),
            pltpu.VMEM((rows, width), f32),
        ],
        pinned=(1, 2),
        smem=(0,),
        far_outs=(0, 1, 2),
    )

    got = exchange(feat_part, "proto")
    (copies,) = on_core(proj_kernel, [shape((n_proto, share, width), bf16)], (got, stud_share))
    proj_grad = exchange(copies, "proto").reshape(rows, width)
    got = lax.ppermute(send, "dp", [(i, i ^ 1) for i in range(16)])
    pair = (keep.astype(f32) + got.astype(f32)).reshape(4, 2, 16, columns)
    quarter = spread_sum(pair, "dp", 0, y_at, lambda i, hop: (i + 4 * hop) % 16, bf16)
    proj_grad, quarter = lax.optimization_barrier((proj_grad, quarter))
    keep = jnp.where(high == 0, quarter[0], quarter[1])
    send = jnp.where(high == 0, quarter[1], quarter[0]).astype(bf16)
    got = lax.ppermute(send, "dp", [(i, i ^ 2) for i in range(16)])
    grad_prototypes = keep + got.astype(f32)
    bottle_part = lax.dot_general(
        proj_grad, student_hidden, (((0,), (0,)), ((), ())), preferred_element_type=f32
    )
    got_bottle = exchange(blocks_of(bottle_part, n_dp), "dp")
    grad_bottleneck = jnp.sum(got_bottle.astype(f32), axis=0).T

    return (grad_prototypes, grad_bottleneck)


def solution(mesh):
    return jax.shard_map(
        on_device,
        mesh=mesh,
        in_specs=(
            P("dp", "proto"),
            P("dp", "proto"),
            P("proto", None),
            P("proto", None),
            P(None, "proto"),
            P(None, "proto"),
        ),
        out_specs=(P("dp", "proto"), P("proto", "dp")),
        check_vma=False,
    )
```
